32 devices in a mesh: grp: 4 (over x, core), sub: 8 (over z, y).
Axes of the slice: x: 2, y: 2, z: 4, core: 2. Of those that a mesh axis runs over, the one named last changes fastest.
Arguments:
- template: bfloat16 [96, 96, 128], P('sub'), may hold values from -4 to 4
- subjects: bfloat16 [32, 96, 96, 128], P(('grp', 'sub')), may hold values from -40 to 40
Outputs:
- velocity: float32 [96, 3, 96, 128], P('sub')
- new_template: float32 [96, 96, 128], P('sub')
- similarity: float32 [], replicated
The draws below stay inside these ranges and needn't reach their ends.
All inputs are finite; a program needn't handle non-finite values.
Results may differ from the reference program's by a relative error of at most 0.0003.
Values may be sent and summed in bfloat16 or wider, within the bound.
A program may use at most 128 MiB of HBM per device.

```python
import math
import jax
import jax.numpy as jnp
from jax import lax

NZ = 96
NX = 96
NY = 128
RADIUS = 4
REACH = 5
SUBJECTS = 32


def joint_fields(key):
    base_key = jax.random.fold_in(key, 101)
    noise_key = jax.random.fold_in(key, 202)
    shift_key = jax.random.fold_in(key, 303)
    sign_key = jax.random.fold_in(key, 404)
    depth = jnp.arange(NZ, dtype=jnp.float32)[:, None, None] / (NZ - 1)
    position = jnp.arange(SUBJECTS, dtype=jnp.float32) / max(SUBJECTS - 1, 1)
    signs = (2 * jax.random.randint(sign_key, (SUBJECTS,), 0, 2) - 1).astype(jnp.float32)
    base = jnp.clip(jax.random.normal(base_key, (NZ, NX, NY), jnp.float32), -4.0, 4.0)
    bias = 1.0 + 2.0 * depth
    spread = 0.4 + 0.6 * depth
    noise = jnp.clip(jax.random.normal(noise_key, (SUBJECTS, NZ, NX, NY), jnp.float32), -4.0, 4.0)
    ratio = 0.5 * 4.0 ** position
    shift = jax.random.uniform(shift_key, (SUBJECTS,), jnp.float32, 0.3, 0.9)
    return (base, bias, spread, noise, ratio, shift, depth, signs)


def draw_template(key, part):
    base, bias, spread, noise, ratio, shift, depth, signs = joint_fields(key)
    return base.astype(jnp.bfloat16)


def draw_subjects(key, part):
    base, bias, spread, noise, ratio, shift, depth, signs = joint_fields(key)
    padded = jnp.pad(base, ((1, 1), (0, 0), (0, 0)))
    slope = (padded[2:] - padded[:-2]) * 0.5
    displacement = shift[:, None, None, None] * (0.2 + 0.8 * depth)[None]
    common = base[None] + displacement * slope[None]
    moved = signs[:, None, None, None] * common + spread[None] * ratio[:, None, None, None] * noise
    return jnp.clip(bias[None] * moved, -40.0, 40.0).astype(jnp.bfloat16)


def setup_inputs(seed: int = 0) -> dict:
    keys = jax.random.split(jax.random.key(seed), 3)
    template = draw_template(jax.random.fold_in(keys[2], 71), 0)
    subjects = draw_subjects(jax.random.fold_in(keys[2], 71), 0)
    return {"template": template, "subjects": subjects}


EPSILON = 1e-05
STEP_LENGTH = 0.5
VARIANCE = 3.0

def shifted_sum(volume, axis, weights):
    extent = (len(weights) - 1) // 2
    widths = [(0, 0), (0, 0), (0, 0)]
    widths[axis] = (extent, extent)
    padded = jnp.pad(volume, widths)
    length = volume.shape[axis]
    result = jnp.zeros_like(volume)
    for offset, weight in enumerate(weights):
        result = result + weight * lax.slice_in_dim(padded, offset, offset + length, axis=axis)
    return result

def filter_all(volume, weights):
    result = shifted_sum(volume, 0, weights)
    result = shifted_sum(result, 1, weights)
    return shifted_sum(result, 2, weights)

def central(volume):
    padded = jnp.pad(volume, 1)
    along_z = (padded[2:, 1:-1, 1:-1] - padded[:-2, 1:-1, 1:-1]) * 0.5
    along_x = (padded[1:-1, 2:, 1:-1] - padded[1:-1, :-2, 1:-1]) * 0.5
    along_y = (padded[1:-1, 1:-1, 2:] - padded[1:-1, 1:-1, :-2]) * 0.5
    return jnp.stack([along_z, along_x, along_y], axis=0)

def reference(template, subjects):
    box_weights = [1.0 / (2 * RADIUS + 1)] * (2 * RADIUS + 1)
    kernel_sum = sum((math.exp(-offset * offset / (2.0 * VARIANCE)) for offset in range(-REACH, REACH + 1)))
    gauss_weights = [math.exp(-offset * offset / (2.0 * VARIANCE)) / kernel_sum for offset in range(-REACH, REACH + 1)]
    cell_count = NZ * NX * NY
    fixed_image = template.astype(jnp.float32)
    mean_i = filter_all(fixed_image, box_weights)
    mean_ii = filter_all(fixed_image * fixed_image, box_weights)
    var_i = mean_ii - mean_i * mean_i
    centred_i = fixed_image - mean_i
    gradients = central(fixed_image)

    def accumulate(carry_state, moving):
        moving = moving.astype(jnp.float32)
        mean_j = filter_all(moving, box_weights)
        mean_jj = filter_all(moving * moving, box_weights)
        mean_ij = filter_all(fixed_image * moving, box_weights)
        cross_sum = mean_ij - mean_i * mean_j
        var_j = mean_jj - mean_j * mean_j
        denominator = var_i * var_j + EPSILON
        factor = 2.0 * cross_sum / denominator * (moving - mean_j - cross_sum / (var_i + EPSILON) * centred_i)
        force_sum, image_sum, cc_sum = carry_state
        return ((force_sum + factor[None] * gradients, image_sum + moving, cc_sum + jnp.sum(cross_sum * cross_sum / denominator)), None)
    initial = (jnp.zeros((3, NZ, NX, NY), jnp.float32), jnp.zeros((NZ, NX, NY), jnp.float32), jnp.zeros((), jnp.float32))
    (force_sum, image_sum, cc_sum), unused = lax.scan(accumulate, initial, subjects)
    smoothed = jnp.stack([filter_all(force_sum[comp], gauss_weights) for comp in range(3)], axis=0)
    mean_velocity = smoothed / SUBJECTS
    mean_image = image_sum / SUBJECTS
    velocity_norm = jnp.sqrt(jnp.sum(mean_velocity * mean_velocity) / cell_count + EPSILON)
    image_norm = jnp.sqrt(jnp.sum(mean_image * mean_image) / cell_count + EPSILON)
    velocity = STEP_LENGTH * mean_velocity / velocity_norm
    normed = mean_image / image_norm
    slopes = central(normed)
    new_template = normed - lax.optimization_barrier(jnp.sum(velocity * slopes, axis=0))
    similarity = cc_sum / (SUBJECTS * cell_count)
    return (jnp.transpose(velocity, (1, 0, 2, 3)), new_template, similarity)
```

```python
import math

import jax
import jax.numpy as jnp
from jax import lax
from jax.experimental import pallas as pl
from jax.experimental.pallas import tpu as pltpu
from jax.sharding import PartitionSpec as P

RADIUS = 4
REACH = 5


EPSILON = 1e-05
STEP_LENGTH = 0.5
VARIANCE = 3.0
HIGH = lax.Precision.HIGHEST


def band_matrix(length, extent, weighted):
    row_ids = lax.broadcasted_iota(jnp.int32, (length, length), 0)
    col_ids = lax.broadcasted_iota(jnp.int32, (length, length), 1)
    inside = jnp.abs(row_ids - col_ids) <= extent
    if weighted:
        offset_f = (row_ids - col_ids).astype(jnp.float32)
        total = sum(math.exp(-o * o / (2.0 * VARIANCE)) for o in range(-extent, extent + 1))
        values = jnp.exp(-offset_f * offset_f / (2.0 * VARIANCE)) / total
        return jnp.where(inside, values, 0.0)
    return jnp.where(inside, 1.0, 0.0).astype(jnp.bfloat16)


def gauss_weights(extent):
    raw = [math.exp(-o * o / (2.0 * VARIANCE)) for o in range(-extent, extent + 1)]
    return [w / sum(raw) for w in raw]


def split_dot(field, band):
    high = field.astype(jnp.bfloat16)
    low = (field - high.astype(jnp.float32)).astype(jnp.bfloat16)
    return jnp.dot(high, band, preferred_element_type=jnp.float32) + jnp.dot(
        low, band, preferred_element_type=jnp.float32
    )


def window_x(plane):
    rows, lanes = plane.shape
    zeros = jnp.zeros((8, lanes), jnp.float32)
    padded = jnp.concatenate([zeros, plane, zeros], axis=0)
    two = padded + pltpu.roll(padded, 1, 0)
    four = two + pltpu.roll(two, 2, 0)
    nine = four + pltpu.roll(four, 4, 0) + pltpu.roll(padded, 8, 0)
    return pltpu.roll(nine, rows + 16 - RADIUS, 0)[8 : 8 + rows]


def factor_kernel(i_ref, j_ref, band_ref, f_ref, cc_ref, sums):
    depth, rows, lanes = i_ref.shape
    chunk = 4
    band = band_ref[...]
    edge = jnp.zeros((RADIUS, rows, lanes), jnp.float32)
    for k in range(5):
        sums[k, :RADIUS] = edge
        sums[k, depth + RADIUS :] = edge
    cc_ref[...] = jnp.zeros_like(cc_ref)

    @pl.loop(0, depth // chunk)
    def _(step):
        z = step * chunk
        i16 = i_ref[pl.ds(z, chunk)].reshape(chunk * rows, lanes)
        j16 = j_ref[pl.ds(z, chunk)].reshape(chunk * rows, lanes)
        i32, j32 = i16.astype(jnp.float32), j16.astype(jnp.float32)
        fields = (
            jnp.dot(i16, band, preferred_element_type=jnp.float32),
            split_dot(i32 * i32, band),
            jnp.dot(j16, band, preferred_element_type=jnp.float32),
            split_dot(j32 * j32, band),
            split_dot(i32 * j32, band),
        )
        for k, field in enumerate(fields):
            sums[k, pl.ds(z + RADIUS, chunk)] = field.reshape(chunk, rows, lanes)

    scale = 1.0 / (2 * RADIUS + 1) ** 3

    @pl.loop(0, depth // chunk)
    def _(step):
        z = step * chunk
        planes = []
        for k in range(5):
            a = [sums[k, z + o] for o in range(chunk + 2 * RADIUS)]
            mid = ((a[3] + a[4]) + (a[5] + a[6])) + (a[7] + a[8])
            p, q = a[1] + a[2], a[9] + a[10]
            outs = (mid + (a[0] + p), mid + (p + a[9]), mid + (a[2] + q), mid + (q + a[11]))
            planes.append([window_x(o) * scale for o in outs])
        for c in range(chunk):
            mean_i, mean_ii, mean_j, mean_jj, mean_ij = (planes[k][c] for k in range(5))
            i32 = i_ref[z + c].astype(jnp.float32)
            j32 = j_ref[z + c].astype(jnp.float32)
            cross = mean_ij - mean_i * mean_j
            var_i = mean_ii - mean_i * mean_i
            var_j = mean_jj - mean_j * mean_j
            ratio = cross / (var_i * var_j + EPSILON)
            slope = cross / (var_i + EPSILON)
            f_ref[z + c] = 2.0 * ratio * (j32 - mean_j - slope * (i32 - mean_i))
            cc_ref[...] += cross * ratio


def factors(image, moving):
    depth, rows, lanes = image.shape
    cells = depth * rows * lanes
    vmem = pl.BlockSpec(memory_space=pltpu.VMEM)
    return pl.pallas_call(
        factor_kernel,
        out_shape=(
            jax.ShapeDtypeStruct((depth, rows, lanes), jnp.float32),
            jax.ShapeDtypeStruct((rows, lanes), jnp.float32),
        ),
        in_specs=[vmem] * 3,
        out_specs=(vmem, vmem),
        scratch_shapes=[pltpu.VMEM((5, depth + 2 * RADIUS, rows, lanes), jnp.float32)],
        compiler_params=pltpu.CompilerParams(vmem_limit_bytes=56 * 2**20),
        cost_estimate=pl.CostEstimate(
            flops=cells * lanes * 16, bytes_accessed=cells * 60, transcendentals=2 * cells
        ),
    )(image, moving, band_matrix(lanes, RADIUS, False))


def with_halo(slab, width):
    devices, length = lax.axis_size("sub"), slab.shape[0]
    before, after = [], []
    hop, left = 1, width
    while left > 0:
        take = min(left, length)
        up = [(i, i + hop) for i in range(devices - hop)]
        down = [(j, i) for i, j in up]
        before.insert(0, lax.ppermute(slab[length - take :], "sub", up))
        after.append(lax.ppermute(slab[:take], "sub", down))
        hop, left = hop + 1, left - take
    return jnp.concatenate(before + [slab] + after, axis=0)


def reduced(volume):
    part = lax.psum_scatter(volume, "grp", scatter_dimension=1, tiled=True)
    part = lax.psum_scatter(part, "sub", scatter_dimension=0, tiled=True)
    return lax.all_gather(part, "grp", axis=1, tiled=True)


def on_device(template, subjects):
    image = lax.all_gather(template, "sub", axis=0, tiled=True)
    depth, height, width = image.shape
    slab = template.shape[0]
    subject_count = subjects.shape[0] * lax.axis_size("grp") * lax.axis_size("sub")
    cell_count = depth * height * width
    mean_image = reduced(subjects[0].astype(jnp.float32)) / subject_count
    padded_mean = with_halo(mean_image, 1)
    factor, cc = factors(image, subjects[0])
    cc_local = jnp.sum(cc)
    total = with_halo(reduced(factor), REACH)

    reach = REACH + 1
    padded = jnp.pad(image, ((reach, reach), (0, 0), (0, 0)))
    near = lax.dynamic_slice_in_dim(padded, lax.axis_index("sub") * slab, slab + 2 * reach, axis=0)
    near = jnp.pad(near.astype(jnp.float32), ((0, 0), (1, 1), (1, 1)))
    slopes = (
        (near[2:, 1:-1, 1:-1] - near[:-2, 1:-1, 1:-1]) * 0.5,
        (near[1:-1, 2:, 1:-1] - near[1:-1, :-2, 1:-1]) * 0.5,
        (near[1:-1, 1:-1, 2:] - near[1:-1, 1:-1, :-2]) * 0.5,
    )
    weights = gauss_weights(REACH)
    along_z = []
    for slope in slopes:
        force = total * slope
        along_z.append(sum(w * force[o : o + slab] for o, w in enumerate(weights)))
    smooth = jnp.stack(along_z, axis=1)
    gauss_x = band_matrix(height, REACH, True)
    gauss_y = band_matrix(width, REACH, True)
    smooth = jnp.einsum(
        "zcxb,ba->zcxa", smooth, gauss_y, precision=HIGH, preferred_element_type=jnp.float32
    )
    smooth = jnp.einsum(
        "ab,zcby->zcay", gauss_x, smooth, precision=HIGH, preferred_element_type=jnp.float32
    )
    mean_velocity = smooth / subject_count
    velocity_square = jnp.sum(mean_velocity * mean_velocity)
    image_square = jnp.sum(mean_image * mean_image)
    groups = lax.axis_size("grp")
    sums = lax.psum(
        jnp.stack([cc_local, velocity_square / groups, image_square / groups]), ("grp", "sub")
    )
    velocity_norm = jnp.sqrt(sums[1] / cell_count + EPSILON)
    image_norm = jnp.sqrt(sums[2] / cell_count + EPSILON)
    velocity = STEP_LENGTH * mean_velocity / velocity_norm
    slope_z = (padded_mean[2:] - padded_mean[:-2]) * 0.5
    padded_x = jnp.pad(mean_image, ((0, 0), (1, 1), (0, 0)))
    slope_x = (padded_x[:, 2:] - padded_x[:, :-2]) * 0.5
    padded_y = jnp.pad(mean_image, ((0, 0), (0, 0), (1, 1)))
    slope_y = (padded_y[:, :, 2:] - padded_y[:, :, :-2]) * 0.5
    advected = velocity[:, 0] * slope_z + velocity[:, 1] * slope_x + velocity[:, 2] * slope_y
    new_template = (mean_image - advected) / image_norm
    similarity = sums[0] / (subject_count * cell_count)
    return (velocity, new_template, similarity)


def solution(mesh):
    placed = (P("sub", None, None), P(("grp", "sub"), None, None, None))
    return jax.shard_map(
        on_device,
        mesh=mesh,
        in_specs=placed,
        out_specs=(P("sub", None, None, None), P("sub", None, None), P()),
        check_vma=False,
    )
```

```python
import functools
import math

import jax
import jax.numpy as jnp
from jax import lax
from jax.experimental import pallas as pl
from jax.experimental.pallas import tpu as pltpu
from jax.sharding import PartitionSpec as P

RADIUS = 4
REACH = 5


EPSILON = 1e-05
STEP_LENGTH = 0.5
VARIANCE = 3.0
HIGH = lax.Precision.HIGHEST
MESH = pl.DeviceIdType.MESH


def band_matrix(length, extent, weighted):
    row_ids = lax.broadcasted_iota(jnp.int32, (length, length), 0)
    col_ids = lax.broadcasted_iota(jnp.int32, (length, length), 1)
    inside = jnp.abs(row_ids - col_ids) <= extent
    if weighted:
        offset_f = (row_ids - col_ids).astype(jnp.float32)
        total = sum(math.exp(-o * o / (2.0 * VARIANCE)) for o in range(-extent, extent + 1))
        values = jnp.exp(-offset_f * offset_f / (2.0 * VARIANCE)) / total
        return jnp.where(inside, values, 0.0)
    return jnp.where(inside, 1.0, 0.0).astype(jnp.bfloat16)


def gauss_weights(extent):
    raw = [math.exp(-o * o / (2.0 * VARIANCE)) for o in range(-extent, extent + 1)]
    return [w / sum(raw) for w in raw]


def split_dot(field, band):
    high = field.astype(jnp.bfloat16)
    low = (field - high.astype(jnp.float32)).astype(jnp.bfloat16)
    return jnp.dot(high, band, preferred_element_type=jnp.float32) + jnp.dot(
        low, band, preferred_element_type=jnp.float32
    )


def window_x(plane):
    rows, lanes = plane.shape
    zeros = jnp.zeros((8, lanes), jnp.float32)
    padded = jnp.concatenate([zeros, plane, zeros], axis=0)
    two = padded + pltpu.roll(padded, 1, 0)
    four = two + pltpu.roll(two, 2, 0)
    nine = four + pltpu.roll(four, 4, 0) + pltpu.roll(padded, 8, 0)
    return pltpu.roll(nine, rows + 16 - RADIUS, 0)[8 : 8 + rows]


def factor_kernel(i_ref, j_ref, band_ref, f_ref, cc_ref, sums):
    depth, rows, lanes = i_ref.shape
    chunk = 4
    band = band_ref[...]
    edge = jnp.zeros((RADIUS, rows, lanes), jnp.float32)
    for k in range(5):
        sums[k, :RADIUS] = edge
        sums[k, depth + RADIUS :] = edge
    cc_ref[...] = jnp.zeros_like(cc_ref)

    @pl.loop(0, depth // chunk)
    def _(step):
        z = step * chunk
        i16 = i_ref[pl.ds(z, chunk)].reshape(chunk * rows, lanes)
        j16 = j_ref[pl.ds(z, chunk)].reshape(chunk * rows, lanes)
        i32, j32 = i16.astype(jnp.float32), j16.astype(jnp.float32)
        fields = (
            jnp.dot(i16, band, preferred_element_type=jnp.float32),
            split_dot(i32 * i32, band),
            jnp.dot(j16, band, preferred_element_type=jnp.float32),
            split_dot(j32 * j32, band),
            split_dot(i32 * j32, band),
        )
        for k, field in enumerate(fields):
            sums[k, pl.ds(z + RADIUS, chunk)] = field.reshape(chunk, rows, lanes)

    scale = 1.0 / (2 * RADIUS + 1) ** 3

    @pl.loop(0, depth // chunk)
    def _(step):
        z = step * chunk
        planes = []
        for k in range(5):
            a = [sums[k, z + o] for o in range(chunk + 2 * RADIUS)]
            mid = ((a[3] + a[4]) + (a[5] + a[6])) + (a[7] + a[8])
            p, q = a[1] + a[2], a[9] + a[10]
            outs = (mid + (a[0] + p), mid + (p + a[9]), mid + (a[2] + q), mid + (q + a[11]))
            planes.append([window_x(o) * scale for o in outs])
        for c in range(chunk):
            mean_i, mean_ii, mean_j, mean_jj, mean_ij = (planes[k][c] for k in range(5))
            i32 = i_ref[z + c].astype(jnp.float32)
            j32 = j_ref[z + c].astype(jnp.float32)
            cross = mean_ij - mean_i * mean_j
            var_i = mean_ii - mean_i * mean_i
            var_j = mean_jj - mean_j * mean_j
            ratio = cross / (var_i * var_j + EPSILON)
            slope = cross / (var_i + EPSILON)
            f_ref[z + c] = 2.0 * ratio * (j32 - mean_j - slope * (i32 - mean_i))
            cc_ref[...] += cross * ratio


def factors(image, moving):
    depth, rows, lanes = image.shape
    cells = depth * rows * lanes
    vmem = pl.BlockSpec(memory_space=pltpu.VMEM)
    return pl.pallas_call(
        factor_kernel,
        out_shape=(
            jax.ShapeDtypeStruct((depth, rows, lanes), jnp.float32),
            jax.ShapeDtypeStruct((rows, lanes), jnp.float32),
        ),
        in_specs=[vmem] * 3,
        out_specs=(vmem, vmem),
        scratch_shapes=[pltpu.VMEM((5, depth + 2 * RADIUS, rows, lanes), jnp.float32)],
        compiler_params=pltpu.CompilerParams(vmem_limit_bytes=56 * 2**20),
        cost_estimate=pl.CostEstimate(
            flops=cells * lanes * 16, bytes_accessed=cells * 60, transcendentals=2 * cells
        ),
    )(image, moving, band_matrix(lanes, RADIUS, False))


def bits(size):
    return [1 << k for k in range(size.bit_length() - 1)]


def plan(groups, owners, order):
    offsets, steps = list(range(owners)), []
    for axis, bit in order:
        if axis == "sub":
            offsets = [o for o in offsets if not o & bit]
        steps.append((axis, bit, offsets))
    return steps


def greet(groups, owners, me):
    g, s = me
    barrier = pltpu.get_barrier_semaphore()
    for r in range(1, groups):
        pl.semaphore_signal(
            barrier, inc=1, device_id=(lax.rem(g + r, groups), s), device_id_type=MESH
        )
    for r in range(1, owners):
        pl.semaphore_signal(
            barrier, inc=1, device_id=(g, lax.rem(s + r, owners)), device_id_type=MESH
        )
    pl.semaphore_wait(barrier, groups + owners - 2)


def bit_of(index, bit):
    return lax.rem(lax.div(index, bit), 2)


class Halving:
    def __init__(self, me, steps, rows, first, acc, recv, send_sem, recv_sem):
        self.me, self.steps, self.first, self.acc = me, steps, first, acc
        self.recv, self.send_sem, self.recv_sem = recv, send_sem, recv_sem
        self.copies = {}
        self.places = []
        base, x0, nx = 0, 0, rows
        count = 0
        g, s = me
        for axis, bit, offsets in steps:
            mine = bit_of(g if axis == "grp" else s, bit)
            flip = bit * (1 - 2 * mine)
            if axis == "grp":
                nx = nx // 2
                aligned = math.gcd(nx, 16)
                away = pl.multiple_of(x0 + (1 - mine) * nx, aligned)
                x0 = pl.multiple_of(x0 + mine * nx, aligned)
                base_away, peer = base, (g + flip, s)
            else:
                away, base_away = x0, base + (1 - mine) * bit
                base, peer = base + mine * bit, (g, s + flip)
            self.places.append((base, base_away, x0, away, nx, peer, mine, count))
            count += len(offsets)

    def send(self, k, i):
        base, base_away, x0, away, nx, peer, mine, count = self.places[k]
        offset = self.steps[k][2][i]
        source = self.first if k == 0 else self.acc
        copy = pltpu.make_async_remote_copy(
            src_ref=source.at[base_away + offset, :, pl.ds(away, nx)],
            dst_ref=self.recv[k].at[i],
            send_sem=self.send_sem.at[count + i],
            recv_sem=self.recv_sem.at[count + i],
            device_id=peer,
            device_id_type=MESH,
        )
        copy.start()
        self.copies[k, i] = copy

    def take(self, k, i):
        base, base_away, x0, away, nx, peer, mine, count = self.places[k]
        offset = self.steps[k][2][i]
        self.copies[k, i].wait_recv()
        source = self.first if k == 0 else self.acc
        here = (base + offset, slice(None), pl.ds(x0, nx))
        self.acc[here] = source[here].astype(jnp.float32) + self.recv[k][i].astype(jnp.float32)

    def send_all(self, k):
        for i in range(len(self.steps[k][2])):
            self.send(k, i)


def reduce_kernel(
    groups, owners, steps_f, steps_m, f_ref, j_ref, total_ref, mean_ref, acc_f, acc_m, slab_f, slab_m, *rest
):
    count = len(steps_f)
    recv_f, recv_m = rest[:count], rest[count : 2 * count]
    f_send, f_recv, m_send, m_recv, g_send, g_recv, h_send, h_recv = rest[2 * count :]
    me = (lax.axis_index("grp"), lax.axis_index("sub"))
    g, s = me
    depth, rows = f_ref.shape[1:3]
    slab_f[...] = jnp.zeros_like(slab_f)
    slab_m[...] = jnp.zeros_like(slab_m)
    greet(groups, owners, me)
    force = Halving(me, steps_f, rows, f_ref, acc_f, recv_f, f_send, f_recv)
    image = Halving(me, steps_m, rows, j_ref, acc_m, recv_m, m_send, m_recv)
    for volume in (force, image):
        volume.send_all(0)
    for k in range(count):
        blocks = [len(v.steps[k][2]) for v in (force, image)]
        for i in range(max(blocks)):
            for volume, n in zip((force, image), blocks):
                if i < n:
                    volume.take(k, i)
                    if k + 1 < count and volume.steps[k + 1][0] == "grp":
                        volume.send(k + 1, i)
        if k + 1 < count:
            for volume in (force, image):
                if volume.steps[k + 1][0] == "sub":
                    volume.send_all(k + 1)
    pending = []
    for n, (volume, slab, edge) in enumerate(((force, slab_f, REACH), (image, slab_m, 1))):
        base, _, x0, _, nx, _, _, _ = volume.places[-1]
        place = (pl.ds(edge, depth), pl.ds(x0, nx))
        slab[place] = volume.acc[base, :, pl.ds(x0, nx)]
        for r in range(1, groups):
            peer_g = g + sum(b * (1 - 2 * bit_of(g, b)) for b in bits(groups) if r & b)
            copy = pltpu.make_async_remote_copy(
                src_ref=slab.at[place],
                dst_ref=slab.at[place],
                send_sem=g_send.at[n * groups + r],
                recv_sem=g_recv.at[n * groups + r],
                device_id=(peer_g, s),
                device_id_type=MESH,
            )
            copy.start()
            pending.append(copy)
    for copy in pending:
        copy.wait_recv()
    halos, at = [], 0
    for slab, edge in ((slab_f, REACH), (slab_m, 1)):
        hop, left = 1, edge
        while left > 0:
            size = min(left, depth)
            near = edge - (hop - 1) * depth
            for up in (True, False):
                step = hop if up else -hop
                source = slab.at[pl.ds(edge + depth - size if up else edge, size)]
                target = slab.at[pl.ds(near - size if up else edge + hop * depth, size)]
                sends = s + hop < owners if up else s >= hop
                receives = s >= hop if up else s + hop < owners
                copy = pltpu.make_async_remote_copy(
                    src_ref=source,
                    dst_ref=target,
                    send_sem=h_send.at[at],
                    recv_sem=h_recv.at[at],
                    device_id=(g, lax.rem(s + step + owners, owners)),
                    device_id_type=MESH,
                )
                pl.when(sends)(copy.start)
                halos.append((copy, sends, receives))
                at += 1
            hop, left = hop + 1, left - size
    for copy, sends, receives in halos:
        pl.when(receives)(copy.wait_recv)
    total_ref[...] = slab_f[...]
    mean_ref[...] = slab_m[...]
    for copy, sends, receives in halos:
        pl.when(sends)(copy.wait_send)
    for copy in pending + list(force.copies.values()) + list(image.copies.values()):
        copy.wait_send()


def reduced(factor, moving):
    groups, owners = lax.axis_size("grp"), lax.axis_size("sub")
    depth, rows, lanes = factor.shape
    slab = depth // owners
    by_group = [("grp", b) for b in bits(groups)]
    by_owner = [("sub", b) for b in bits(owners)]
    order_f = by_group + by_owner
    order_m = by_group[:1] + by_owner[:1] + by_group[1:] + by_owner[1:]
    steps_f, steps_m = plan(groups, owners, order_f), plan(groups, owners, order_m)
    recv = []
    for n, steps in enumerate((steps_f, steps_m)):
        nx = rows
        for k, (axis, _, offsets) in enumerate(steps):
            nx = nx // 2 if axis == "grp" else nx
            kind = jnp.bfloat16 if n == 1 and k == 0 else jnp.float32
            recv.append(pltpu.VMEM((len(offsets), slab, nx, lanes), kind))
    copies = [sum(len(o) for _, _, o in steps) for steps in (steps_f, steps_m)]
    halos = 2 * (-(-REACH // slab)) + 2
    dma = pltpu.SemaphoreType.DMA
    vmem = pl.BlockSpec(memory_space=pltpu.VMEM)
    shape_f, shape_m = (slab + 2 * REACH, rows, lanes), (slab + 2, rows, lanes)
    blocks = (owners, slab, rows, lanes)
    return pl.pallas_call(
        functools.partial(reduce_kernel, groups, owners, steps_f, steps_m),
        out_shape=tuple(jax.ShapeDtypeStruct(x, jnp.float32) for x in (shape_f, shape_m)),
        in_specs=[vmem] * 2,
        out_specs=(vmem, vmem),
        scratch_shapes=[
            pltpu.VMEM(blocks, jnp.float32),
            pltpu.VMEM(blocks, jnp.float32),
            pltpu.VMEM(shape_f, jnp.float32),
            pltpu.VMEM(shape_m, jnp.float32),
            *recv,
            dma((copies[0],)),
            dma((copies[0],)),
            dma((copies[1],)),
            dma((copies[1],)),
            dma((2 * groups,)),
            dma((2 * groups,)),
            dma((halos,)),
            dma((halos,)),
        ],
        compiler_params=pltpu.CompilerParams(
            collective_id=1, has_side_effects=True, vmem_limit_bytes=56 * 2**20
        ),
    )(factor.reshape(blocks), moving.reshape(blocks))


def sum_kernel(groups, owners, in_ref, out_ref, row, column, send_sem, recv_sem):
    me = (lax.axis_index("grp"), lax.axis_index("sub"))
    g, s = me
    greet(groups, owners, me)
    at, copies = 0, []
    row[0] = in_ref[...]
    for axis, size, slots in (("grp", groups, row), ("sub", owners, column)):
        started = []
        for r in range(1, size):
            peer = (lax.rem(g + r, size), s) if axis == "grp" else (g, lax.rem(s + r, size))
            copy = pltpu.make_async_remote_copy(
                src_ref=slots.at[0],
                dst_ref=slots.at[r],
                send_sem=send_sem.at[at],
                recv_sem=recv_sem.at[at],
                device_id=peer,
                device_id_type=MESH,
            )
            copy.start()
            started.append(copy)
            at += 1
        for copy in started:
            copy.wait_recv()
        copies += started
        mine = g if axis == "grp" else s
        total = slots[lax.rem(mine + size, size)]
        for rank in range(1, size):
            total = total + slots[lax.rem(mine - rank + size, size)]
        if axis == "grp":
            column[0] = total
        else:
            out_ref[...] = total
    for copy in copies:
        copy.wait_send()


def summed(values):
    groups, owners = lax.axis_size("grp"), lax.axis_size("sub")
    copies = groups + owners - 2
    vmem = pl.BlockSpec(memory_space=pltpu.VMEM)
    shape = (8, 128)
    rows = jnp.pad(jnp.stack(values), (0, 8 - len(values)))
    out = pl.pallas_call(
        functools.partial(sum_kernel, groups, owners),
        out_shape=jax.ShapeDtypeStruct(shape, jnp.float32),
        in_specs=[vmem],
        out_specs=vmem,
        scratch_shapes=[
            pltpu.VMEM((groups, *shape), jnp.float32),
            pltpu.VMEM((owners, *shape), jnp.float32),
            pltpu.SemaphoreType.DMA((copies,)),
            pltpu.SemaphoreType.DMA((copies,)),
        ],
        compiler_params=pltpu.CompilerParams(collective_id=2, has_side_effects=True),
    )(jnp.broadcast_to(rows[:, None], shape))
    return [out[k, 0] for k in range(len(values))]


def on_device(template, subjects):
    image = lax.all_gather(template, "sub", axis=0, tiled=True)
    depth, height, width = image.shape
    slab = template.shape[0]
    subject_count = subjects.shape[0] * lax.axis_size("grp") * lax.axis_size("sub")
    cell_count = depth * height * width
    factor, cc = factors(image, subjects[0])
    cc_local = jnp.sum(cc)
    total, image_sum = reduced(factor, subjects[0])
    padded_mean = image_sum / subject_count
    mean_image = padded_mean[1:-1]

    reach = REACH + 1
    padded = jnp.pad(image, ((reach, reach), (0, 0), (0, 0)))
    near = lax.dynamic_slice_in_dim(padded, lax.axis_index("sub") * slab, slab + 2 * reach, axis=0)
    near = jnp.pad(near.astype(jnp.float32), ((0, 0), (1, 1), (1, 1)))
    slopes = (
        (near[2:, 1:-1, 1:-1] - near[:-2, 1:-1, 1:-1]) * 0.5,
        (near[1:-1, 2:, 1:-1] - near[1:-1, :-2, 1:-1]) * 0.5,
        (near[1:-1, 1:-1, 2:] - near[1:-1, 1:-1, :-2]) * 0.5,
    )
    weights = gauss_weights(REACH)
    along_z = []
    for slope in slopes:
        force = total * slope
        along_z.append(sum(w * force[o : o + slab] for o, w in enumerate(weights)))
    smooth = jnp.stack(along_z, axis=1)
    gauss_x = band_matrix(height, REACH, True)
    gauss_y = band_matrix(width, REACH, True)
    smooth = jnp.einsum(
        "zcxb,ba->zcxa", smooth, gauss_y, precision=HIGH, preferred_element_type=jnp.float32
    )
    smooth = jnp.einsum(
        "ab,zcby->zcay", gauss_x, smooth, precision=HIGH, preferred_element_type=jnp.float32
    )
    mean_velocity = smooth / subject_count
    velocity_square = jnp.sum(mean_velocity * mean_velocity)
    image_square = jnp.sum(mean_image * mean_image)
    groups = lax.axis_size("grp")
    sums = summed([cc_local, velocity_square / groups, image_square / groups])
    velocity_norm = jnp.sqrt(sums[1] / cell_count + EPSILON)
    image_norm = jnp.sqrt(sums[2] / cell_count + EPSILON)
    velocity = STEP_LENGTH * mean_velocity / velocity_norm
    slope_z = (padded_mean[2:] - padded_mean[:-2]) * 0.5
    padded_x = jnp.pad(mean_image, ((0, 0), (1, 1), (0, 0)))
    slope_x = (padded_x[:, 2:] - padded_x[:, :-2]) * 0.5
    padded_y = jnp.pad(mean_image, ((0, 0), (0, 0), (1, 1)))
    slope_y = (padded_y[:, :, 2:] - padded_y[:, :, :-2]) * 0.5
    advected = velocity[:, 0] * slope_z + velocity[:, 1] * slope_x + velocity[:, 2] * slope_y
    new_template = (mean_image - advected) / image_norm
    similarity = sums[0] / (subject_count * cell_count)
    return (velocity, new_template, similarity)


def solution(mesh):
    placed = (P("sub", None, None), P(("grp", "sub"), None, None, None))
    return jax.shard_map(
        on_device,
        mesh=mesh,
        in_specs=placed,
        out_specs=(P("sub", None, None, None), P("sub", None, None), P()),
        check_vma=False,
    )
```

```python
import functools
import math

import jax
import jax.numpy as jnp
from jax import lax
from jax.experimental import pallas as pl
from jax.experimental.pallas import tpu as pltpu
from jax.sharding import PartitionSpec as P

RADIUS = 4
REACH = 5


EPSILON = 1e-05
STEP_LENGTH = 0.5
VARIANCE = 3.0
HIGH = lax.Precision.HIGHEST
MESH = pl.DeviceIdType.MESH


def band_matrix(length, extent, weighted):
    row_ids = lax.broadcasted_iota(jnp.int32, (length, length), 0)
    col_ids = lax.broadcasted_iota(jnp.int32, (length, length), 1)
    inside = jnp.abs(row_ids - col_ids) <= extent
    if weighted:
        offset_f = (row_ids - col_ids).astype(jnp.float32)
        total = sum(math.exp(-o * o / (2.0 * VARIANCE)) for o in range(-extent, extent + 1))
        values = jnp.exp(-offset_f * offset_f / (2.0 * VARIANCE)) / total
        return jnp.where(inside, values, 0.0)
    return jnp.where(inside, 1.0, 0.0).astype(jnp.bfloat16)


def gauss_weights(extent):
    raw = [math.exp(-o * o / (2.0 * VARIANCE)) for o in range(-extent, extent + 1)]
    return [w / sum(raw) for w in raw]


def split_dot(field, band):
    high = field.astype(jnp.bfloat16)
    low = (field - high.astype(jnp.float32)).astype(jnp.bfloat16)
    return jnp.dot(high, band, preferred_element_type=jnp.float32) + jnp.dot(
        low, band, preferred_element_type=jnp.float32
    )


def window_x(plane):
    rows, lanes = plane.shape
    zeros = jnp.zeros((8, lanes), jnp.float32)
    padded = jnp.concatenate([zeros, plane, zeros], axis=0)
    two = padded + pltpu.roll(padded, 1, 0)
    four = two + pltpu.roll(two, 2, 0)
    nine = four + pltpu.roll(four, 4, 0) + pltpu.roll(padded, 8, 0)
    return pltpu.roll(nine, rows + 16 - RADIUS, 0)[8 : 8 + rows]


def row_sums(i_ref, j_ref, band_ref, sums):
    owners, slab, rows, lanes = i_ref.shape
    depth = owners * slab
    band = band_ref[...]
    edge = jnp.zeros((RADIUS, rows, lanes), jnp.float32)
    for k in range(5):
        sums[k, :RADIUS] = edge
        sums[k, depth + RADIUS :] = edge

    @pl.loop(0, owners)
    def _(block):
        for z0 in range(0, slab, 3):
            size = min(3, slab - z0)
            i16 = i_ref[block, z0 : z0 + size].reshape(size * rows, lanes)
            j16 = j_ref[block, z0 : z0 + size].reshape(size * rows, lanes)
            i32, j32 = i16.astype(jnp.float32), j16.astype(jnp.float32)
            fields = (
                jnp.dot(i16, band, preferred_element_type=jnp.float32),
                split_dot(i32 * i32, band),
                jnp.dot(j16, band, preferred_element_type=jnp.float32),
                split_dot(j32 * j32, band),
                split_dot(i32 * j32, band),
            )
            for k, field in enumerate(fields):
                place = pl.ds(block * slab + z0 + RADIUS, size)
                sums[k, place] = field.reshape(size, rows, lanes)


def window_z(a):
    if len(a) == 4 + 2 * RADIUS:
        mid = ((a[3] + a[4]) + (a[5] + a[6])) + (a[7] + a[8])
        p, q = a[1] + a[2], a[9] + a[10]
        return (mid + (a[0] + p), mid + (p + a[9]), mid + (a[2] + q), mid + (q + a[11]))
    return [sum(a[c + 1 : c + 2 * RADIUS + 1], a[c]) for c in range(len(a) - 2 * RADIUS)]


def block_factors(first, last, i_ref, j_ref, f_ref, cc_ref, sums):
    slab = i_ref.shape[1]
    chunk = 4 if slab % 4 == 0 else 1
    scale = 1.0 / (2 * RADIUS + 1) ** 3
    parts = slab // chunk

    @pl.loop(first * parts, last * parts)
    def _(step):
        block, z0 = lax.div(step, parts), lax.rem(step, parts) * chunk
        planes = []
        for k in range(5):
            a = [sums[k, step * chunk + o] for o in range(chunk + 2 * RADIUS)]
            planes.append([window_x(o) * scale for o in window_z(a)])
        for c in range(chunk):
            mean_i, mean_ii, mean_j, mean_jj, mean_ij = (planes[k][c] for k in range(5))
            i32 = i_ref[block, z0 + c].astype(jnp.float32)
            j32 = j_ref[block, z0 + c].astype(jnp.float32)
            cross = mean_ij - mean_i * mean_j
            var_i = mean_ii - mean_i * mean_i
            var_j = mean_jj - mean_j * mean_j
            ratio = cross / (var_i * var_j + EPSILON)
            slope = cross / (var_i + EPSILON)
            f_ref[block, z0 + c] = 2.0 * ratio * (j32 - mean_j - slope * (i32 - mean_i))
            cc_ref[...] += cross * ratio


def bits(size):
    return [1 << k for k in range(size.bit_length() - 1)]


def plan(groups, owners, order):
    offsets, steps = list(range(owners)), []
    for axis, bit in order:
        if axis == "sub":
            offsets = [o for o in offsets if not o & bit]
        steps.append((axis, bit, offsets))
    return steps


def greet(groups, owners, me):
    g, s = me
    barrier = pltpu.get_barrier_semaphore()
    for r in range(1, groups):
        pl.semaphore_signal(
            barrier, inc=1, device_id=(lax.rem(g + r, groups), s), device_id_type=MESH
        )
    for r in range(1, owners):
        pl.semaphore_signal(
            barrier, inc=1, device_id=(g, lax.rem(s + r, owners)), device_id_type=MESH
        )
    pl.semaphore_wait(barrier, groups + owners - 2)


def bit_of(index, bit):
    return lax.rem(lax.div(index, bit), 2)


class Halving:
    def __init__(self, me, steps, rows, first, acc, recv, send_sem, recv_sem):
        self.me, self.steps, self.first, self.acc = me, steps, first, acc
        self.recv, self.send_sem, self.recv_sem = recv, send_sem, recv_sem
        self.copies = {}
        self.places = []
        base, x0, nx = 0, 0, rows
        count = 0
        g, s = me
        for axis, bit, offsets in steps:
            mine = bit_of(g if axis == "grp" else s, bit)
            flip = bit * (1 - 2 * mine)
            if axis == "grp":
                nx = nx // 2
                aligned = math.gcd(nx, 16)
                away = pl.multiple_of(x0 + (1 - mine) * nx, aligned)
                x0 = pl.multiple_of(x0 + mine * nx, aligned)
                base_away, peer = base, (g + flip, s)
            else:
                away, base_away = x0, base + (1 - mine) * bit
                base, peer = base + mine * bit, (g, s + flip)
            self.places.append((base, base_away, x0, away, nx, peer, mine, count))
            count += len(offsets)

    def send(self, k, i):
        base, base_away, x0, away, nx, peer, mine, count = self.places[k]
        offset = self.steps[k][2][i]
        source = self.first if k == 0 else self.acc
        copy = pltpu.make_async_remote_copy(
            src_ref=source.at[base_away + offset, :, pl.ds(away, nx)],
            dst_ref=self.recv[k].at[i],
            send_sem=self.send_sem.at[count + i],
            recv_sem=self.recv_sem.at[count + i],
            device_id=peer,
            device_id_type=MESH,
        )
        copy.start()
        self.copies[k, i] = copy

    def take(self, k, i):
        base, base_away, x0, away, nx, peer, mine, count = self.places[k]
        offset = self.steps[k][2][i]
        self.copies[k, i].wait_recv()
        source = self.first if k == 0 else self.acc
        here = (base + offset, slice(None), pl.ds(x0, nx))
        self.acc[here] = source[here].astype(jnp.float32) + self.recv[k][i].astype(jnp.float32)

    def pass_on(self, k, i):
        self.take(k, i)
        if k + 1 < len(self.steps) and self.steps[k + 1][0] == "grp":
            self.send(k + 1, i)

    def finish(self, k):
        if k + 1 < len(self.steps) and self.steps[k + 1][0] == "sub":
            self.send_all(k + 1)

    def advance(self, k):
        for i in range(len(self.steps[k][2])):
            self.pass_on(k, i)
        self.finish(k)

    def send_all(self, k):
        for i in range(len(self.steps[k][2])):
            self.send(k, i)


def reduce_kernel(
    groups,
    owners,
    steps_f,
    steps_m,
    i_ref,
    j_ref,
    band_ref,
    total_ref,
    mean_ref,
    cc_ref,
    sums,
    acc_f,
    acc_m,
    slab_f,
    slab_m,
    *rest,
):
    count = len(steps_f)
    recv_f, recv_m = rest[:count], rest[count : 2 * count]
    f_send, f_recv, m_send, m_recv, g_send, g_recv, h_send, h_recv = rest[2 * count :]
    me = (lax.axis_index("grp"), lax.axis_index("sub"))
    g, s = me
    depth, rows = j_ref.shape[1:3]
    slab_f[...] = jnp.zeros_like(slab_f)
    slab_m[...] = jnp.zeros_like(slab_m)
    greet(groups, owners, me)
    force = Halving(me, steps_f, rows, acc_f, acc_f, recv_f, f_send, f_recv)
    image = Halving(me, steps_m, rows, j_ref, acc_m, recv_m, m_send, m_recv)
    image.send_all(0)
    cc_ref[...] = jnp.zeros_like(cc_ref)
    row_sums(i_ref, j_ref, band_ref, sums)
    image.advance(0)
    lead = [owners * k // (count - 1) for k in range(count)]
    waiting = []
    for k in range(1, count):
        first, last = lead[k - 1], lead[k]
        block_factors(first, last, i_ref, j_ref, acc_f, cc_ref, sums)
        for i in range(first, last):
            force.send(0, i)
        image.advance(k)
        for i in waiting:
            force.pass_on(0, i)
        waiting = range(first, last)
    for i in waiting:
        force.pass_on(0, i)
    force.finish(0)
    for k in range(1, count):
        force.advance(k)
    pending = []
    for n, (volume, slab, edge) in enumerate(((force, slab_f, REACH), (image, slab_m, 1))):
        base, _, x0, _, nx, _, _, _ = volume.places[-1]
        place = (pl.ds(edge, depth), pl.ds(x0, nx))
        slab[place] = volume.acc[base, :, pl.ds(x0, nx)]
        for r in range(1, groups):
            peer_g = g + sum(b * (1 - 2 * bit_of(g, b)) for b in bits(groups) if r & b)
            copy = pltpu.make_async_remote_copy(
                src_ref=slab.at[place],
                dst_ref=slab.at[place],
                send_sem=g_send.at[n * groups + r],
                recv_sem=g_recv.at[n * groups + r],
                device_id=(peer_g, s),
                device_id_type=MESH,
            )
            copy.start()
            pending.append(copy)
    for copy in pending:
        copy.wait_recv()
    halos, at = [], 0
    for slab, edge in ((slab_f, REACH), (slab_m, 1)):
        hop, left = 1, edge
        while left > 0:
            size = min(left, depth)
            near = edge - (hop - 1) * depth
            for up in (True, False):
                step = hop if up else -hop
                source = slab.at[pl.ds(edge + depth - size if up else edge, size)]
                target = slab.at[pl.ds(near - size if up else edge + hop * depth, size)]
                sends = s + hop < owners if up else s >= hop
                receives = s >= hop if up else s + hop < owners
                copy = pltpu.make_async_remote_copy(
                    src_ref=source,
                    dst_ref=target,
                    send_sem=h_send.at[at],
                    recv_sem=h_recv.at[at],
                    device_id=(g, lax.rem(s + step + owners, owners)),
                    device_id_type=MESH,
                )
                pl.when(sends)(copy.start)
                halos.append((copy, sends, receives))
                at += 1
            hop, left = hop + 1, left - size
    for copy, sends, receives in halos:
        pl.when(receives)(copy.wait_recv)
    total_ref[...] = slab_f[...]
    mean_ref[...] = slab_m[...]
    for copy, sends, receives in halos:
        pl.when(sends)(copy.wait_send)
    for copy in pending + list(force.copies.values()) + list(image.copies.values()):
        copy.wait_send()


def reduced(image, moving):
    groups, owners = lax.axis_size("grp"), lax.axis_size("sub")
    depth, rows, lanes = moving.shape
    slab = depth // owners
    by_group = [("grp", b) for b in bits(groups)]
    by_owner = [("sub", b) for b in bits(owners)]
    order_f = by_group + by_owner
    order_m = by_group[:1] + by_owner[:1] + by_group[1:] + by_owner[1:]
    steps_f, steps_m = plan(groups, owners, order_f), plan(groups, owners, order_m)
    recv = []
    for n, steps in enumerate((steps_f, steps_m)):
        nx = rows
        for k, (axis, _, offsets) in enumerate(steps):
            nx = nx // 2 if axis == "grp" else nx
            kind = jnp.bfloat16 if n == 1 and k == 0 else jnp.float32
            recv.append(pltpu.VMEM((len(offsets), slab, nx, lanes), kind))
    copies = [sum(len(o) for _, _, o in steps) for steps in (steps_f, steps_m)]
    halos = 2 * (-(-REACH // slab)) + 2
    dma = pltpu.SemaphoreType.DMA
    vmem = pl.BlockSpec(memory_space=pltpu.VMEM)
    shape_f, shape_m = (slab + 2 * REACH, rows, lanes), (slab + 2, rows, lanes)
    blocks = (owners, slab, rows, lanes)
    return pl.pallas_call(
        functools.partial(reduce_kernel, groups, owners, steps_f, steps_m),
        out_shape=tuple(
            jax.ShapeDtypeStruct(x, jnp.float32) for x in (shape_f, shape_m, (rows, lanes))
        ),
        in_specs=[vmem] * 3,
        out_specs=(vmem,) * 3,
        scratch_shapes=[
            pltpu.VMEM((5, depth + 2 * RADIUS, rows, lanes), jnp.float32),
            pltpu.VMEM(blocks, jnp.float32),
            pltpu.VMEM(blocks, jnp.float32),
            pltpu.VMEM(shape_f, jnp.float32),
            pltpu.VMEM(shape_m, jnp.float32),
            *recv,
            dma((copies[0],)),
            dma((copies[0],)),
            dma((copies[1],)),
            dma((copies[1],)),
            dma((2 * groups,)),
            dma((2 * groups,)),
            dma((halos,)),
            dma((halos,)),
        ],
        compiler_params=pltpu.CompilerParams(
            collective_id=1, has_side_effects=True, vmem_limit_bytes=60 * 2**20
        ),
    )(image.reshape(blocks), moving.reshape(blocks), band_matrix(lanes, RADIUS, False))


def sum_kernel(groups, owners, in_ref, out_ref, row, column, send_sem, recv_sem):
    me = (lax.axis_index("grp"), lax.axis_index("sub"))
    g, s = me
    greet(groups, owners, me)
    at, copies = 0, []
    row[0] = in_ref[...]
    for axis, size, slots in (("grp", groups, row), ("sub", owners, column)):
        started = []
        for r in range(1, size):
            peer = (lax.rem(g + r, size), s) if axis == "grp" else (g, lax.rem(s + r, size))
            copy = pltpu.make_async_remote_copy(
                src_ref=slots.at[0],
                dst_ref=slots.at[r],
                send_sem=send_sem.at[at],
                recv_sem=recv_sem.at[at],
                device_id=peer,
                device_id_type=MESH,
            )
            copy.start()
            started.append(copy)
            at += 1
        for copy in started:
            copy.wait_recv()
        copies += started
        mine = g if axis == "grp" else s
        total = slots[lax.rem(mine + size, size)]
        for rank in range(1, size):
            total = total + slots[lax.rem(mine - rank + size, size)]
        if axis == "grp":
            column[0] = total
        else:
            out_ref[...] = total
    for copy in copies:
        copy.wait_send()


def summed(values):
    groups, owners = lax.axis_size("grp"), lax.axis_size("sub")
    copies = groups + owners - 2
    vmem = pl.BlockSpec(memory_space=pltpu.VMEM)
    shape = (8, 128)
    rows = jnp.pad(jnp.stack(values), (0, 8 - len(values)))
    out = pl.pallas_call(
        functools.partial(sum_kernel, groups, owners),
        out_shape=jax.ShapeDtypeStruct(shape, jnp.float32),
        in_specs=[vmem],
        out_specs=vmem,
        scratch_shapes=[
            pltpu.VMEM((groups, *shape), jnp.float32),
            pltpu.VMEM((owners, *shape), jnp.float32),
            pltpu.SemaphoreType.DMA((copies,)),
            pltpu.SemaphoreType.DMA((copies,)),
        ],
        compiler_params=pltpu.CompilerParams(collective_id=2, has_side_effects=True),
    )(jnp.broadcast_to(rows[:, None], shape))
    return [out[k, 0] for k in range(len(values))]


def gather_kernel(groups, owners, t_ref, out_ref, whole, send_sem, recv_sem):
    me = (lax.axis_index("grp"), lax.axis_index("sub"))
    g, s = me
    half = t_ref.shape[1] // 2
    core = bit_of(g, 1)
    whole[s] = t_ref[...]
    greet(groups, owners, me)
    x0 = pl.multiple_of(core * half, math.gcd(half, 16))
    at, copies, across = 0, [], []

    def start(block, peer):
        nonlocal at
        place = whole.at[block, :, pl.ds(x0, half)]
        copy = pltpu.make_async_remote_copy(
            src_ref=place,
            dst_ref=place,
            send_sem=send_sem.at[at],
            recv_sem=recv_sem.at[at],
            device_id=peer,
            device_id_type=MESH,
        )
        copy.start()
        copies.append(copy)
        at += 1
        return copy

    def flipped(pattern):
        return s + sum(b * (1 - 2 * bit_of(s, b)) for b in bits(owners) if pattern & b)

    held = [0]
    for bit in reversed(bits(owners)):
        started = [start(flipped(p), (g, flipped(bit))) for p in held]
        for p, copy in zip(held, started):
            copy.wait_recv()
            across.append(start(flipped(p | bit), (g + 1 - 2 * core, s)))
        held = held + [p | bit for p in held]
    for copy in across:
        copy.wait_recv()
    out_ref[...] = whole[...]
    for copy in copies:
        copy.wait_send()


def gathered(template):
    groups, owners = lax.axis_size("grp"), lax.axis_size("sub")
    vmem = pl.BlockSpec(memory_space=pltpu.VMEM)
    shape = (owners, *template.shape)
    copies = 2 * (owners - 1)
    return pl.pallas_call(
        functools.partial(gather_kernel, groups, owners),
        out_shape=jax.ShapeDtypeStruct(shape, template.dtype),
        in_specs=[vmem],
        out_specs=vmem,
        scratch_shapes=[
            pltpu.VMEM(shape, template.dtype),
            pltpu.SemaphoreType.DMA((copies,)),
            pltpu.SemaphoreType.DMA((copies,)),
        ],
        compiler_params=pltpu.CompilerParams(
            collective_id=3, has_side_effects=True, vmem_limit_bytes=32 * 2**20
        ),
    )(template).reshape(-1, *template.shape[1:])


def on_device(template, subjects):
    image = gathered(template)
    depth, height, width = image.shape
    slab = template.shape[0]
    subject_count = subjects.shape[0] * lax.axis_size("grp") * lax.axis_size("sub")
    cell_count = depth * height * width
    total, image_sum, cc = reduced(image, subjects[0])
    cc_local = jnp.sum(cc)
    padded_mean = image_sum / subject_count
    mean_image = padded_mean[1:-1]

    reach = REACH + 1
    padded = jnp.pad(image, ((reach, reach), (0, 0), (0, 0)))
    near = lax.dynamic_slice_in_dim(padded, lax.axis_index("sub") * slab, slab + 2 * reach, axis=0)
    near = jnp.pad(near.astype(jnp.float32), ((0, 0), (1, 1), (1, 1)))
    slopes = (
        (near[2:, 1:-1, 1:-1] - near[:-2, 1:-1, 1:-1]) * 0.5,
        (near[1:-1, 2:, 1:-1] - near[1:-1, :-2, 1:-1]) * 0.5,
        (near[1:-1, 1:-1, 2:] - near[1:-1, 1:-1, :-2]) * 0.5,
    )
    weights = gauss_weights(REACH)
    along_z = []
    for slope in slopes:
        force = total * slope
        along_z.append(sum(w * force[o : o + slab] for o, w in enumerate(weights)))
    smooth = jnp.stack(along_z, axis=1)
    gauss_x = band_matrix(height, REACH, True)
    gauss_y = band_matrix(width, REACH, True)
    smooth = jnp.einsum(
        "zcxb,ba->zcxa", smooth, gauss_y, precision=HIGH, preferred_element_type=jnp.float32
    )
    smooth = jnp.einsum(
        "ab,zcby->zcay", gauss_x, smooth, precision=HIGH, preferred_element_type=jnp.float32
    )
    mean_velocity = smooth / subject_count
    velocity_square = jnp.sum(mean_velocity * mean_velocity)
    image_square = jnp.sum(mean_image * mean_image)
    groups = lax.axis_size("grp")
    sums = summed([cc_local, velocity_square / groups, image_square / groups])
    velocity_norm = jnp.sqrt(sums[1] / cell_count + EPSILON)
    image_norm = jnp.sqrt(sums[2] / cell_count + EPSILON)
    velocity = STEP_LENGTH * mean_velocity / velocity_norm
    slope_z = (padded_mean[2:] - padded_mean[:-2]) * 0.5
    padded_x = jnp.pad(mean_image, ((0, 0), (1, 1), (0, 0)))
    slope_x = (padded_x[:, 2:] - padded_x[:, :-2]) * 0.5
    padded_y = jnp.pad(mean_image, ((0, 0), (0, 0), (1, 1)))
    slope_y = (padded_y[:, :, 2:] - padded_y[:, :, :-2]) * 0.5
    advected = velocity[:, 0] * slope_z + velocity[:, 1] * slope_x + velocity[:, 2] * slope_y
    new_template = (mean_image - advected) / image_norm
    similarity = sums[0] / (subject_count * cell_count)
    return (velocity, new_template, similarity)


def solution(mesh):
    placed = (P("sub", None, None), P(("grp", "sub"), None, None, None))
    return jax.shard_map(
        on_device,
        mesh=mesh,
        in_specs=placed,
        out_specs=(P("sub", None, None, None), P("sub", None, None), P()),
        check_vma=False,
    )
```

```python
import functools
import math

import jax
import jax.numpy as jnp
from jax import lax
from jax.experimental import pallas as pl
from jax.experimental.pallas import tpu as pltpu
from jax.sharding import PartitionSpec as P

RADIUS = 4
REACH = 5


EPSILON = 1e-05
STEP_LENGTH = 0.5
VARIANCE = 3.0
HIGH = lax.Precision.HIGHEST
MESH = pl.DeviceIdType.MESH


def band_matrix(length, extent, weighted):
    row_ids = lax.broadcasted_iota(jnp.int32, (length, length), 0)
    col_ids = lax.broadcasted_iota(jnp.int32, (length, length), 1)
    inside = jnp.abs(row_ids - col_ids) <= extent
    if weighted:
        offset_f = (row_ids - col_ids).astype(jnp.float32)
        total = sum(math.exp(-o * o / (2.0 * VARIANCE)) for o in range(-extent, extent + 1))
        values = jnp.exp(-offset_f * offset_f / (2.0 * VARIANCE)) / total
        return jnp.where(inside, values, 0.0)
    return jnp.where(inside, 1.0, 0.0).astype(jnp.bfloat16)


def gauss_weights(extent):
    raw = [math.exp(-o * o / (2.0 * VARIANCE)) for o in range(-extent, extent + 1)]
    return [w / sum(raw) for w in raw]


def split_dot(field, band):
    high = field.astype(jnp.bfloat16)
    low = (field - high.astype(jnp.float32)).astype(jnp.bfloat16)
    return jnp.dot(high, band, preferred_element_type=jnp.float32) + jnp.dot(
        low, band, preferred_element_type=jnp.float32
    )


def window_x(plane):
    rows, lanes = plane.shape
    zeros = jnp.zeros((8, lanes), jnp.float32)
    padded = jnp.concatenate([zeros, plane, zeros], axis=0)
    two = padded + pltpu.roll(padded, 1, 0)
    four = two + pltpu.roll(two, 2, 0)
    nine = four + pltpu.roll(four, 4, 0) + pltpu.roll(padded, 8, 0)
    return pltpu.roll(nine, rows + 16 - RADIUS, 0)[8 : 8 + rows]


def row_sums(i_ref, j_ref, band_ref, sums):
    owners, slab, rows, lanes = i_ref.shape
    depth = owners * slab
    band = band_ref[...]
    edge = jnp.zeros((RADIUS, rows, lanes), jnp.float32)
    for k in range(5):
        sums[k, :RADIUS] = edge
        sums[k, depth + RADIUS :] = edge

    @pl.loop(0, owners)
    def _(block):
        for z0 in range(0, slab, 3):
            size = min(3, slab - z0)
            i16 = i_ref[block, z0 : z0 + size].reshape(size * rows, lanes)
            j16 = j_ref[block, z0 : z0 + size].reshape(size * rows, lanes)
            i32, j32 = i16.astype(jnp.float32), j16.astype(jnp.float32)
            fields = (
                jnp.dot(i16, band, preferred_element_type=jnp.float32),
                split_dot(i32 * i32, band),
                jnp.dot(j16, band, preferred_element_type=jnp.float32),
                split_dot(j32 * j32, band),
                split_dot(i32 * j32, band),
            )
            for k, field in enumerate(fields):
                place = pl.ds(block * slab + z0 + RADIUS, size)
                sums[k, place] = field.reshape(size, rows, lanes)


def window_z(a):
    if len(a) == 4 + 2 * RADIUS:
        mid = ((a[3] + a[4]) + (a[5] + a[6])) + (a[7] + a[8])
        p, q = a[1] + a[2], a[9] + a[10]
        return (mid + (a[0] + p), mid + (p + a[9]), mid + (a[2] + q), mid + (q + a[11]))
    return [sum(a[c + 1 : c + 2 * RADIUS + 1], a[c]) for c in range(len(a) - 2 * RADIUS)]


def block_factors(first, last, i_ref, j_ref, f_ref, cc_ref, sums):
    slab = i_ref.shape[1]
    chunk = 4 if slab % 4 == 0 else 1
    scale = 1.0 / (2 * RADIUS + 1) ** 3
    parts = slab // chunk

    @pl.loop(first * parts, last * parts)
    def _(step):
        block, z0 = lax.div(step, parts), lax.rem(step, parts) * chunk
        planes = []
        for k in range(5):
            a = [sums[k, step * chunk + o] for o in range(chunk + 2 * RADIUS)]
            planes.append([window_x(o) * scale for o in window_z(a)])
        for c in range(chunk):
            mean_i, mean_ii, mean_j, mean_jj, mean_ij = (planes[k][c] for k in range(5))
            i32 = i_ref[block, z0 + c].astype(jnp.float32)
            j32 = j_ref[block, z0 + c].astype(jnp.float32)
            cross = mean_ij - mean_i * mean_j
            var_i = mean_ii - mean_i * mean_i
            var_j = mean_jj - mean_j * mean_j
            ratio = cross / (var_i * var_j + EPSILON)
            slope = cross / (var_i + EPSILON)
            f_ref[block, z0 + c] = 2.0 * ratio * (j32 - mean_j - slope * (i32 - mean_i))
            cc_ref[...] += cross * ratio


def bits(size):
    return [1 << k for k in range(size.bit_length() - 1)]


def plan(groups, owners, order):
    offsets, steps = list(range(owners)), []
    for axis, bit in order:
        if axis == "sub":
            offsets = [o for o in offsets if not o & bit]
        steps.append((axis, bit, offsets))
    return steps


def greet(groups, owners, me):
    g, s = me
    barrier = pltpu.get_barrier_semaphore()
    for r in range(1, groups):
        pl.semaphore_signal(
            barrier, inc=1, device_id=(lax.rem(g + r, groups), s), device_id_type=MESH
        )
    for r in range(1, owners):
        pl.semaphore_signal(
            barrier, inc=1, device_id=(g, lax.rem(s + r, owners)), device_id_type=MESH
        )
    pl.semaphore_wait(barrier, groups + owners - 2)


def bit_of(index, bit):
    return lax.rem(lax.div(index, bit), 2)


class Halving:
    def __init__(self, me, steps, rows, first, acc, recv, send_sem, recv_sem):
        self.me, self.steps, self.first, self.acc = me, steps, first, acc
        self.recv, self.send_sem, self.recv_sem = recv, send_sem, recv_sem
        self.copies = {}
        self.places = []
        base, x0, nx = 0, 0, rows
        count = 0
        g, s = me
        for axis, bit, offsets in steps:
            mine = bit_of(g if axis == "grp" else s, bit)
            flip = bit * (1 - 2 * mine)
            if axis == "grp":
                nx = nx // 2
                aligned = math.gcd(nx, 16)
                away = pl.multiple_of(x0 + (1 - mine) * nx, aligned)
                x0 = pl.multiple_of(x0 + mine * nx, aligned)
                base_away, peer = base, (g + flip, s)
            else:
                away, base_away = x0, base + (1 - mine) * bit
                base, peer = base + mine * bit, (g, s + flip)
            self.places.append((base, base_away, x0, away, nx, peer, mine, count))
            count += len(offsets)

    def send(self, k, i):
        base, base_away, x0, away, nx, peer, mine, count = self.places[k]
        offset = self.steps[k][2][i]
        source = self.first if k == 0 else self.acc
        copy = pltpu.make_async_remote_copy(
            src_ref=source.at[base_away + offset, :, pl.ds(away, nx)],
            dst_ref=self.recv[k].at[i],
            send_sem=self.send_sem.at[count + i],
            recv_sem=self.recv_sem.at[count + i],
            device_id=peer,
            device_id_type=MESH,
        )
        copy.start()
        self.copies[k, i] = copy

    def take(self, k, i):
        base, base_away, x0, away, nx, peer, mine, count = self.places[k]
        offset = self.steps[k][2][i]
        self.copies[k, i].wait_recv()
        source = self.first if k == 0 else self.acc
        here = (base + offset, slice(None), pl.ds(x0, nx))
        self.acc[here] = source[here].astype(jnp.float32) + self.recv[k][i].astype(jnp.float32)

    def pass_on(self, k, i):
        self.take(k, i)
        if k + 1 < len(self.steps) and self.steps[k + 1][0] == "grp":
            self.send(k + 1, i)

    def finish(self, k):
        if k + 1 < len(self.steps) and self.steps[k + 1][0] == "sub":
            self.send_all(k + 1)

    def advance(self, k):
        for i in range(len(self.steps[k][2])):
            self.pass_on(k, i)
        self.finish(k)

    def send_all(self, k):
        for i in range(len(self.steps[k][2])):
            self.send(k, i)


def reduce_kernel(
    groups,
    owners,
    steps_f,
    steps_m,
    i_ref,
    j_ref,
    band_ref,
    total_ref,
    mean_ref,
    cc_ref,
    sums,
    acc_f,
    acc_m,
    slab_f,
    slab_m,
    *rest,
):
    count = len(steps_f)
    recv_f, recv_m = rest[:count], rest[count : 2 * count]
    f_send, f_recv, m_send, m_recv, g_send, g_recv, h_send, h_recv = rest[2 * count :]
    me = (lax.axis_index("grp"), lax.axis_index("sub"))
    g, s = me
    depth, rows = j_ref.shape[1:3]
    slab_f[...] = jnp.zeros_like(slab_f)
    slab_m[...] = jnp.zeros_like(slab_m)
    greet(groups, owners, me)
    force = Halving(me, steps_f, rows, acc_f, acc_f, recv_f, f_send, f_recv)
    image = Halving(me, steps_m, rows, j_ref, acc_m, recv_m, m_send, m_recv)
    image.send_all(0)
    cc_ref[...] = jnp.zeros_like(cc_ref)
    row_sums(i_ref, j_ref, band_ref, sums)
    image.advance(0)
    lead = [owners * k // (count - 1) for k in range(count)]
    waiting = []
    for k in range(1, count):
        first, last = lead[k - 1], lead[k]
        block_factors(first, last, i_ref, j_ref, acc_f, cc_ref, sums)
        for i in range(first, last):
            force.send(0, i)
        for i in waiting:
            force.pass_on(0, i)
        waiting = range(first, last)
    for i in waiting:
        force.pass_on(0, i)
    force.finish(0)
    for k in range(1, count):
        image.advance(k)
        if k > 1:
            force.advance(k - 1)
    force.advance(count - 1)
    pending = []
    for n, (volume, slab, edge) in enumerate(((force, slab_f, REACH), (image, slab_m, 1))):
        base, _, x0, _, nx, _, _, _ = volume.places[-1]
        place = (pl.ds(edge, depth), pl.ds(x0, nx))
        slab[place] = volume.acc[base, :, pl.ds(x0, nx)]
        for r in range(1, groups):
            peer_g = g + sum(b * (1 - 2 * bit_of(g, b)) for b in bits(groups) if r & b)
            copy = pltpu.make_async_remote_copy(
                src_ref=slab.at[place],
                dst_ref=slab.at[place],
                send_sem=g_send.at[n * groups + r],
                recv_sem=g_recv.at[n * groups + r],
                device_id=(peer_g, s),
                device_id_type=MESH,
            )
            copy.start()
            pending.append(copy)
    for copy in pending:
        copy.wait_recv()
    halos, at = [], 0
    for slab, edge in ((slab_f, REACH), (slab_m, 1)):
        hop, left = 1, edge
        while left > 0:
            size = min(left, depth)
            near = edge - (hop - 1) * depth
            for up in (True, False):
                step = hop if up else -hop
                source = slab.at[pl.ds(edge + depth - size if up else edge, size)]
                target = slab.at[pl.ds(near - size if up else edge + hop * depth, size)]
                sends = s + hop < owners if up else s >= hop
                receives = s >= hop if up else s + hop < owners
                copy = pltpu.make_async_remote_copy(
                    src_ref=source,
                    dst_ref=target,
                    send_sem=h_send.at[at],
                    recv_sem=h_recv.at[at],
                    device_id=(g, lax.rem(s + step + owners, owners)),
                    device_id_type=MESH,
                )
                pl.when(sends)(copy.start)
                halos.append((copy, sends, receives))
                at += 1
            hop, left = hop + 1, left - size
    for copy, sends, receives in halos:
        pl.when(receives)(copy.wait_recv)
    total_ref[...] = slab_f[...]
    mean_ref[...] = slab_m[...]
    for copy, sends, receives in halos:
        pl.when(sends)(copy.wait_send)
    for copy in pending + list(force.copies.values()) + list(image.copies.values()):
        copy.wait_send()


def reduced(image, moving):
    groups, owners = lax.axis_size("grp"), lax.axis_size("sub")
    depth, rows, lanes = moving.shape
    slab = depth // owners
    by_group = [("grp", b) for b in bits(groups)]
    by_owner = [("sub", b) for b in bits(owners)]
    order_f = by_group + by_owner
    order_m = by_group[:1] + by_owner + by_group[1:]
    steps_f, steps_m = plan(groups, owners, order_f), plan(groups, owners, order_m)
    recv = []
    for n, steps in enumerate((steps_f, steps_m)):
        nx = rows
        for k, (axis, _, offsets) in enumerate(steps):
            nx = nx // 2 if axis == "grp" else nx
            kind = jnp.bfloat16 if n == 1 and k == 0 else jnp.float32
            recv.append(pltpu.VMEM((len(offsets), slab, nx, lanes), kind))
    copies = [sum(len(o) for _, _, o in steps) for steps in (steps_f, steps_m)]
    halos = 2 * (-(-REACH // slab)) + 2
    dma = pltpu.SemaphoreType.DMA
    vmem = pl.BlockSpec(memory_space=pltpu.VMEM)
    shape_f, shape_m = (slab + 2 * REACH, rows, lanes), (slab + 2, rows, lanes)
    blocks = (owners, slab, rows, lanes)
    return pl.pallas_call(
        functools.partial(reduce_kernel, groups, owners, steps_f, steps_m),
        out_shape=tuple(
            jax.ShapeDtypeStruct(x, jnp.float32) for x in (shape_f, shape_m, (rows, lanes))
        ),
        in_specs=[vmem] * 3,
        out_specs=(vmem,) * 3,
        scratch_shapes=[
            pltpu.VMEM((5, depth + 2 * RADIUS, rows, lanes), jnp.float32),
            pltpu.VMEM(blocks, jnp.float32),
            pltpu.VMEM(blocks, jnp.float32),
            pltpu.VMEM(shape_f, jnp.float32),
            pltpu.VMEM(shape_m, jnp.float32),
            *recv,
            dma((copies[0],)),
            dma((copies[0],)),
            dma((copies[1],)),
            dma((copies[1],)),
            dma((2 * groups,)),
            dma((2 * groups,)),
            dma((halos,)),
            dma((halos,)),
        ],
        compiler_params=pltpu.CompilerParams(
            collective_id=1, has_side_effects=True, vmem_limit_bytes=60 * 2**20
        ),
    )(image.reshape(blocks), moving.reshape(blocks), band_matrix(lanes, RADIUS, False))


def sum_kernel(groups, owners, in_ref, out_ref, row, column, send_sem, recv_sem):
    me = (lax.axis_index("grp"), lax.axis_index("sub"))
    g, s = me
    greet(groups, owners, me)
    at, copies = 0, []
    row[0] = in_ref[...]
    for axis, size, slots in (("grp", groups, row), ("sub", owners, column)):
        started = []
        for r in range(1, size):
            peer = (lax.rem(g + r, size), s) if axis == "grp" else (g, lax.rem(s + r, size))
            copy = pltpu.make_async_remote_copy(
                src_ref=slots.at[0],
                dst_ref=slots.at[r],
                send_sem=send_sem.at[at],
                recv_sem=recv_sem.at[at],
                device_id=peer,
                device_id_type=MESH,
            )
            copy.start()
            started.append(copy)
            at += 1
        for copy in started:
            copy.wait_recv()
        copies += started
        mine = g if axis == "grp" else s
        total = slots[lax.rem(mine + size, size)]
        for rank in range(1, size):
            total = total + slots[lax.rem(mine - rank + size, size)]
        if axis == "grp":
            column[0] = total
        else:
            out_ref[...] = total
    for copy in copies:
        copy.wait_send()


def summed(values):
    groups, owners = lax.axis_size("grp"), lax.axis_size("sub")
    copies = groups + owners - 2
    vmem = pl.BlockSpec(memory_space=pltpu.VMEM)
    shape = (8, 128)
    rows = jnp.pad(jnp.stack(values), (0, 8 - len(values)))
    out = pl.pallas_call(
        functools.partial(sum_kernel, groups, owners),
        out_shape=jax.ShapeDtypeStruct(shape, jnp.float32),
        in_specs=[vmem],
        out_specs=vmem,
        scratch_shapes=[
            pltpu.VMEM((groups, *shape), jnp.float32),
            pltpu.VMEM((owners, *shape), jnp.float32),
            pltpu.SemaphoreType.DMA((copies,)),
            pltpu.SemaphoreType.DMA((copies,)),
        ],
        compiler_params=pltpu.CompilerParams(collective_id=2, has_side_effects=True),
    )(jnp.broadcast_to(rows[:, None], shape))
    return [out[k, 0] for k in range(len(values))]


def gather_kernel(groups, owners, t_ref, out_ref, whole, send_sem, recv_sem):
    me = (lax.axis_index("grp"), lax.axis_index("sub"))
    g, s = me
    half = t_ref.shape[1] // 2
    core = bit_of(g, 1)
    whole[s] = t_ref[...]
    greet(groups, owners, me)
    x0 = pl.multiple_of(core * half, math.gcd(half, 16))
    at, copies, across = 0, [], []

    def start(block, peer):
        nonlocal at
        place = whole.at[block, :, pl.ds(x0, half)]
        copy = pltpu.make_async_remote_copy(
            src_ref=place,
            dst_ref=place,
            send_sem=send_sem.at[at],
            recv_sem=recv_sem.at[at],
            device_id=peer,
            device_id_type=MESH,
        )
        copy.start()
        copies.append(copy)
        at += 1
        return copy

    def flipped(pattern):
        return s + sum(b * (1 - 2 * bit_of(s, b)) for b in bits(owners) if pattern & b)

    held = [0]
    for bit in reversed(bits(owners)):
        started = [start(flipped(p), (g, flipped(bit))) for p in held]
        for p, copy in zip(held, started):
            copy.wait_recv()
            across.append(start(flipped(p | bit), (g + 1 - 2 * core, s)))
        held = held + [p | bit for p in held]
    for copy in across:
        copy.wait_recv()
    out_ref[...] = whole[...]
    for copy in copies:
        copy.wait_send()


def gathered(template):
    groups, owners = lax.axis_size("grp"), lax.axis_size("sub")
    vmem = pl.BlockSpec(memory_space=pltpu.VMEM)
    shape = (owners, *template.shape)
    copies = 2 * (owners - 1)
    return pl.pallas_call(
        functools.partial(gather_kernel, groups, owners),
        out_shape=jax.ShapeDtypeStruct(shape, template.dtype),
        in_specs=[vmem],
        out_specs=vmem,
        scratch_shapes=[
            pltpu.VMEM(shape, template.dtype),
            pltpu.SemaphoreType.DMA((copies,)),
            pltpu.SemaphoreType.DMA((copies,)),
        ],
        compiler_params=pltpu.CompilerParams(
            collective_id=3, has_side_effects=True, vmem_limit_bytes=32 * 2**20
        ),
    )(template).reshape(-1, *template.shape[1:])


def on_device(template, subjects):
    image = gathered(template)
    depth, height, width = image.shape
    slab = template.shape[0]
    subject_count = subjects.shape[0] * lax.axis_size("grp") * lax.axis_size("sub")
    cell_count = depth * height * width
    total, image_sum, cc = reduced(image, subjects[0])
    cc_local = jnp.sum(cc)
    padded_mean = image_sum / subject_count
    mean_image = padded_mean[1:-1]

    reach = REACH + 1
    padded = jnp.pad(image, ((reach, reach), (0, 0), (0, 0)))
    near = lax.dynamic_slice_in_dim(padded, lax.axis_index("sub") * slab, slab + 2 * reach, axis=0)
    near = jnp.pad(near.astype(jnp.float32), ((0, 0), (1, 1), (1, 1)))
    slopes = (
        (near[2:, 1:-1, 1:-1] - near[:-2, 1:-1, 1:-1]) * 0.5,
        (near[1:-1, 2:, 1:-1] - near[1:-1, :-2, 1:-1]) * 0.5,
        (near[1:-1, 1:-1, 2:] - near[1:-1, 1:-1, :-2]) * 0.5,
    )
    weights = gauss_weights(REACH)
    along_z = []
    for slope in slopes:
        force = total * slope
        along_z.append(sum(w * force[o : o + slab] for o, w in enumerate(weights)))
    smooth = jnp.stack(along_z, axis=1)
    gauss_x = band_matrix(height, REACH, True)
    gauss_y = band_matrix(width, REACH, True)
    smooth = jnp.einsum(
        "zcxb,ba->zcxa", smooth, gauss_y, precision=HIGH, preferred_element_type=jnp.float32
    )
    smooth = jnp.einsum(
        "ab,zcby->zcay", gauss_x, smooth, precision=HIGH, preferred_element_type=jnp.float32
    )
    mean_velocity = smooth / subject_count
    velocity_square = jnp.sum(mean_velocity * mean_velocity)
    image_square = jnp.sum(mean_image * mean_image)
    groups = lax.axis_size("grp")
    sums = summed([cc_local, velocity_square / groups, image_square / groups])
    velocity_norm = jnp.sqrt(sums[1] / cell_count + EPSILON)
    image_norm = jnp.sqrt(sums[2] / cell_count + EPSILON)
    velocity = STEP_LENGTH * mean_velocity / velocity_norm
    slope_z = (padded_mean[2:] - padded_mean[:-2]) * 0.5
    padded_x = jnp.pad(mean_image, ((0, 0), (1, 1), (0, 0)))
    slope_x = (padded_x[:, 2:] - padded_x[:, :-2]) * 0.5
    padded_y = jnp.pad(mean_image, ((0, 0), (0, 0), (1, 1)))
    slope_y = (padded_y[:, :, 2:] - padded_y[:, :, :-2]) * 0.5
    advected = velocity[:, 0] * slope_z + velocity[:, 1] * slope_x + velocity[:, 2] * slope_y
    new_template = (mean_image - advected) / image_norm
    similarity = sums[0] / (subject_count * cell_count)
    return (velocity, new_template, similarity)


def solution(mesh):
    placed = (P("sub", None, None), P(("grp", "sub"), None, None, None))
    return jax.shard_map(
        on_device,
        mesh=mesh,
        in_specs=placed,
        out_specs=(P("sub", None, None, None), P("sub", None, None), P()),
        check_vma=False,
    )
```

```python
import functools
import math

import jax
import jax.numpy as jnp
from jax import lax
from jax.experimental import pallas as pl
from jax.experimental.pallas import tpu as pltpu
from jax.sharding import PartitionSpec as P

RADIUS = 4
REACH = 5


EPSILON = 1e-05
STEP_LENGTH = 0.5
VARIANCE = 3.0
HIGH = lax.Precision.HIGHEST
MESH = pl.DeviceIdType.MESH


def band_matrix(length, extent, weighted):
    row_ids = lax.broadcasted_iota(jnp.int32, (length, length), 0)
    col_ids = lax.broadcasted_iota(jnp.int32, (length, length), 1)
    inside = jnp.abs(row_ids - col_ids) <= extent
    if weighted:
        offset_f = (row_ids - col_ids).astype(jnp.float32)
        total = sum(math.exp(-o * o / (2.0 * VARIANCE)) for o in range(-extent, extent + 1))
        values = jnp.exp(-offset_f * offset_f / (2.0 * VARIANCE)) / total
        return jnp.where(inside, values, 0.0)
    return jnp.where(inside, 1.0, 0.0).astype(jnp.bfloat16)


def gauss_weights(extent):
    raw = [math.exp(-o * o / (2.0 * VARIANCE)) for o in range(-extent, extent + 1)]
    return [w / sum(raw) for w in raw]


def split_dot(field, band):
    high = field.astype(jnp.bfloat16)
    low = (field - high.astype(jnp.float32)).astype(jnp.bfloat16)
    return jnp.dot(high, band, preferred_element_type=jnp.float32) + jnp.dot(
        low, band, preferred_element_type=jnp.float32
    )


def window_x(plane):
    rows, lanes = plane.shape
    zeros = jnp.zeros((8, lanes), jnp.float32)
    padded = jnp.concatenate([zeros, plane, zeros], axis=0)
    two = padded + pltpu.roll(padded, 1, 0)
    four = two + pltpu.roll(two, 2, 0)
    nine = four + pltpu.roll(four, 4, 0) + pltpu.roll(padded, 8, 0)
    return pltpu.roll(nine, rows + 16 - RADIUS, 0)[8 : 8 + rows]


def row_sums(i_ref, j_ref, band_ref, sums):
    owners, slab, rows, lanes = i_ref.shape
    depth = owners * slab
    band = band_ref[...]
    edge = jnp.zeros((RADIUS, rows, lanes), jnp.float32)
    for k in range(5):
        sums[k, :RADIUS] = edge
        sums[k, depth + RADIUS :] = edge

    @pl.loop(0, owners)
    def _(block):
        for z0 in range(0, slab, 3):
            size = min(3, slab - z0)
            i16 = i_ref[block, z0 : z0 + size].reshape(size * rows, lanes)
            j16 = j_ref[block, z0 : z0 + size].reshape(size * rows, lanes)
            i32, j32 = i16.astype(jnp.float32), j16.astype(jnp.float32)
            fields = (
                jnp.dot(i16, band, preferred_element_type=jnp.float32),
                split_dot(i32 * i32, band),
                jnp.dot(j16, band, preferred_element_type=jnp.float32),
                split_dot(j32 * j32, band),
                split_dot(i32 * j32, band),
            )
            for k, field in enumerate(fields):
                place = pl.ds(block * slab + z0 + RADIUS, size)
                sums[k, place] = field.reshape(size, rows, lanes)


def window_z(a):
    if len(a) == 4 + 2 * RADIUS:
        mid = ((a[3] + a[4]) + (a[5] + a[6])) + (a[7] + a[8])
        p, q = a[1] + a[2], a[9] + a[10]
        return (mid + (a[0] + p), mid + (p + a[9]), mid + (a[2] + q), mid + (q + a[11]))
    return [sum(a[c + 1 : c + 2 * RADIUS + 1], a[c]) for c in range(len(a) - 2 * RADIUS)]


def block_factors(first, last, i_ref, j_ref, f_ref, cc_ref, sums):
    slab = i_ref.shape[1]
    chunk = 4 if slab % 4 == 0 else 1
    scale = 1.0 / (2 * RADIUS + 1) ** 3
    parts = slab // chunk

    @pl.loop(first * parts, last * parts)
    def _(step):
        block, z0 = lax.div(step, parts), lax.rem(step, parts) * chunk
        planes = []
        for k in range(5):
            a = [sums[k, step * chunk + o] for o in range(chunk + 2 * RADIUS)]
            planes.append([window_x(o) * scale for o in window_z(a)])
        for c in range(chunk):
            mean_i, mean_ii, mean_j, mean_jj, mean_ij = (planes[k][c] for k in range(5))
            i32 = i_ref[block, z0 + c].astype(jnp.float32)
            j32 = j_ref[block, z0 + c].astype(jnp.float32)
            cross = mean_ij - mean_i * mean_j
            var_i = mean_ii - mean_i * mean_i
            var_j = mean_jj - mean_j * mean_j
            ratio = cross / (var_i * var_j + EPSILON)
            slope = cross / (var_i + EPSILON)
            f_ref[block, z0 + c] = 2.0 * ratio * (j32 - mean_j - slope * (i32 - mean_i))
            cc_ref[...] += cross * ratio


def bits(size):
    return [1 << k for k in range(size.bit_length() - 1)]


def plan(groups, owners, order):
    offsets, steps = list(range(owners)), []
    for axis, bit in order:
        if axis == "sub":
            offsets = [o for o in offsets if not o & bit]
        steps.append((axis, bit, offsets))
    return steps


def greet(groups, owners, me):
    g, s = me
    barrier = pltpu.get_barrier_semaphore()
    for r in range(1, groups):
        pl.semaphore_signal(
            barrier, inc=1, device_id=(lax.rem(g + r, groups), s), device_id_type=MESH
        )
    for r in range(1, owners):
        pl.semaphore_signal(
            barrier, inc=1, device_id=(g, lax.rem(s + r, owners)), device_id_type=MESH
        )
    pl.semaphore_wait(barrier, groups + owners - 2)


def bit_of(index, bit):
    return lax.rem(lax.div(index, bit), 2)


class Halving:
    def __init__(self, me, steps, rows, first, acc, recv, send_sem, recv_sem):
        self.me, self.steps, self.first, self.acc = me, steps, first, acc
        self.recv, self.send_sem, self.recv_sem = recv, send_sem, recv_sem
        self.copies = {}
        self.places = []
        base, x0, nx = 0, 0, rows
        count = 0
        g, s = me
        for axis, bit, offsets in steps:
            mine = bit_of(g if axis == "grp" else s, bit)
            flip = bit * (1 - 2 * mine)
            if axis == "grp":
                nx = nx // 2
                aligned = math.gcd(nx, 16)
                away = pl.multiple_of(x0 + (1 - mine) * nx, aligned)
                x0 = pl.multiple_of(x0 + mine * nx, aligned)
                base_away, peer = base, (g + flip, s)
            else:
                away, base_away = x0, base + (1 - mine) * bit
                base, peer = base + mine * bit, (g, s + flip)
            self.places.append((base, base_away, x0, away, nx, peer, mine, count))
            count += len(offsets)

    def send(self, k, i):
        base, base_away, x0, away, nx, peer, mine, count = self.places[k]
        offset = self.steps[k][2][i]
        source = self.first if k == 0 else self.acc
        copy = pltpu.make_async_remote_copy(
            src_ref=source.at[base_away + offset, :, pl.ds(away, nx)],
            dst_ref=self.recv[k].at[i],
            send_sem=self.send_sem.at[count + i],
            recv_sem=self.recv_sem.at[count + i],
            device_id=peer,
            device_id_type=MESH,
        )
        copy.start()
        self.copies[k, i] = copy

    def take(self, k, i):
        base, base_away, x0, away, nx, peer, mine, count = self.places[k]
        offset = self.steps[k][2][i]
        self.copies[k, i].wait_recv()
        source = self.first if k == 0 else self.acc
        here = (base + offset, slice(None), pl.ds(x0, nx))
        self.acc[here] = source[here].astype(jnp.float32) + self.recv[k][i].astype(jnp.float32)

    def pass_on(self, k, i):
        self.take(k, i)
        if k + 1 < len(self.steps) and self.steps[k + 1][0] == "grp":
            self.send(k + 1, i)

    def finish(self, k):
        if k + 1 < len(self.steps) and self.steps[k + 1][0] == "sub":
            self.send_all(k + 1)

    def advance(self, k):
        for i in range(len(self.steps[k][2])):
            self.pass_on(k, i)
        self.finish(k)

    def send_all(self, k):
        for i in range(len(self.steps[k][2])):
            self.send(k, i)


def reduce_kernel(
    groups,
    owners,
    steps_f,
    steps_m,
    i_ref,
    j_ref,
    band_ref,
    total_ref,
    mean_ref,
    cc_ref,
    sums,
    acc_f,
    acc_m,
    slab_f,
    slab_m,
    *rest,
):
    count = len(steps_f)
    recv_f, recv_m = rest[:count], rest[count : 2 * count]
    f_send, f_recv, m_send, m_recv, g_send, g_recv, h_send, h_recv = rest[2 * count :]
    me = (lax.axis_index("grp"), lax.axis_index("sub"))
    g, s = me
    depth, rows = j_ref.shape[1:3]
    slab_f[...] = jnp.zeros_like(slab_f)
    slab_m[...] = jnp.zeros_like(slab_m)
    greet(groups, owners, me)
    force = Halving(me, steps_f, rows, acc_f, acc_f, recv_f, f_send, f_recv)
    image = Halving(me, steps_m, rows, j_ref, acc_m, recv_m, m_send, m_recv)
    image.send_all(0)
    cc_ref[...] = jnp.zeros_like(cc_ref)
    row_sums(i_ref, j_ref, band_ref, sums)
    image.advance(0)
    lead = [owners * k // (count - 1) for k in range(count)]
    waiting = []
    for k in range(1, count):
        first, last = lead[k - 1], lead[k]
        block_factors(first, last, i_ref, j_ref, acc_f, cc_ref, sums)
        for i in range(first, last):
            force.send(0, i)
        for i in waiting:
            force.pass_on(0, i)
        waiting = range(first, last)
    for i in waiting:
        force.pass_on(0, i)
    force.finish(0)
    for k in range(1, count):
        image.advance(k)
        if k > 1:
            force.advance(k - 1)
    pending = []
    for n, (volume, slab, edge) in enumerate(((image, slab_m, 1), (force, slab_f, REACH))):
        if n == 1:
            force.advance(count - 1)
        base, _, x0, _, nx, _, _, _ = volume.places[-1]
        place = (pl.ds(edge, depth), pl.ds(x0, nx))
        slab[place] = volume.acc[base, :, pl.ds(x0, nx)]
        for r in range(1, groups):
            peer_g = g + sum(b * (1 - 2 * bit_of(g, b)) for b in bits(groups) if r & b)
            copy = pltpu.make_async_remote_copy(
                src_ref=slab.at[place],
                dst_ref=slab.at[place],
                send_sem=g_send.at[n * groups + r],
                recv_sem=g_recv.at[n * groups + r],
                device_id=(peer_g, s),
                device_id_type=MESH,
            )
            copy.start()
            pending.append(copy)
    for copy in pending:
        copy.wait_recv()
    halos, at = [], 0
    for slab, edge in ((slab_f, REACH), (slab_m, 1)):
        hop, left = 1, edge
        while left > 0:
            size = min(left, depth)
            near = edge - (hop - 1) * depth
            for up in (True, False):
                step = hop if up else -hop
                source = slab.at[pl.ds(edge + depth - size if up else edge, size)]
                target = slab.at[pl.ds(near - size if up else edge + hop * depth, size)]
                sends = s + hop < owners if up else s >= hop
                receives = s >= hop if up else s + hop < owners
                copy = pltpu.make_async_remote_copy(
                    src_ref=source,
                    dst_ref=target,
                    send_sem=h_send.at[at],
                    recv_sem=h_recv.at[at],
                    device_id=(g, lax.rem(s + step + owners, owners)),
                    device_id_type=MESH,
                )
                pl.when(sends)(copy.start)
                halos.append((copy, sends, receives))
                at += 1
            hop, left = hop + 1, left - size
    for copy, sends, receives in halos:
        pl.when(receives)(copy.wait_recv)
    total_ref[...] = slab_f[...]
    mean_ref[...] = slab_m[...]
    for copy, sends, receives in halos:
        pl.when(sends)(copy.wait_send)
    for copy in pending + list(force.copies.values()) + list(image.copies.values()):
        copy.wait_send()


def reduced(image, moving):
    groups, owners = lax.axis_size("grp"), lax.axis_size("sub")
    depth, rows, lanes = moving.shape
    slab = depth // owners
    by_group = [("grp", b) for b in bits(groups)]
    by_owner = [("sub", b) for b in bits(owners)]
    order_f = by_group + by_owner
    order_m = by_group[:1] + by_owner + by_group[1:]
    steps_f, steps_m = plan(groups, owners, order_f), plan(groups, owners, order_m)
    recv = []
    for n, steps in enumerate((steps_f, steps_m)):
        nx = rows
        for k, (axis, _, offsets) in enumerate(steps):
            nx = nx // 2 if axis == "grp" else nx
            kind = jnp.bfloat16 if n == 1 and k == 0 else jnp.float32
            recv.append(pltpu.VMEM((len(offsets), slab, nx, lanes), kind))
    copies = [sum(len(o) for _, _, o in steps) for steps in (steps_f, steps_m)]
    halos = 2 * (-(-REACH // slab)) + 2
    dma = pltpu.SemaphoreType.DMA
    vmem = pl.BlockSpec(memory_space=pltpu.VMEM)
    shape_f, shape_m = (slab + 2 * REACH, rows, lanes), (slab + 2, rows, lanes)
    blocks = (owners, slab, rows, lanes)
    return pl.pallas_call(
        functools.partial(reduce_kernel, groups, owners, steps_f, steps_m),
        out_shape=tuple(
            jax.ShapeDtypeStruct(x, jnp.float32) for x in (shape_f, shape_m, (rows, lanes))
        ),
        in_specs=[vmem] * 3,
        out_specs=(vmem,) * 3,
        scratch_shapes=[
            pltpu.VMEM((5, depth + 2 * RADIUS, rows, lanes), jnp.float32),
            pltpu.VMEM(blocks, jnp.float32),
            pltpu.VMEM(blocks, jnp.float32),
            pltpu.VMEM(shape_f, jnp.float32),
            pltpu.VMEM(shape_m, jnp.float32),
            *recv,
            dma((copies[0],)),
            dma((copies[0],)),
            dma((copies[1],)),
            dma((copies[1],)),
            dma((2 * groups,)),
            dma((2 * groups,)),
            dma((halos,)),
            dma((halos,)),
        ],
        compiler_params=pltpu.CompilerParams(
            collective_id=1, has_side_effects=True, vmem_limit_bytes=60 * 2**20
        ),
    )(image.reshape(blocks), moving.reshape(blocks), band_matrix(lanes, RADIUS, False))


def sum_kernel(groups, owners, in_ref, out_ref, row, column, send_sem, recv_sem):
    me = (lax.axis_index("grp"), lax.axis_index("sub"))
    g, s = me
    greet(groups, owners, me)
    at, copies = 0, []
    row[0] = in_ref[...]
    for axis, size, slots in (("grp", groups, row), ("sub", owners, column)):
        started = []
        for r in range(1, size):
            peer = (lax.rem(g + r, size), s) if axis == "grp" else (g, lax.rem(s + r, size))
            copy = pltpu.make_async_remote_copy(
                src_ref=slots.at[0],
                dst_ref=slots.at[r],
                send_sem=send_sem.at[at],
                recv_sem=recv_sem.at[at],
                device_id=peer,
                device_id_type=MESH,
            )
            copy.start()
            started.append(copy)
            at += 1
        for copy in started:
            copy.wait_recv()
        copies += started
        mine = g if axis == "grp" else s
        total = slots[lax.rem(mine + size, size)]
        for rank in range(1, size):
            total = total + slots[lax.rem(mine - rank + size, size)]
        if axis == "grp":
            column[0] = total
        else:
            out_ref[...] = total
    for copy in copies:
        copy.wait_send()


def summed(values):
    groups, owners = lax.axis_size("grp"), lax.axis_size("sub")
    copies = groups + owners - 2
    vmem = pl.BlockSpec(memory_space=pltpu.VMEM)
    shape = (8, 128)
    rows = jnp.pad(jnp.stack(values), (0, 8 - len(values)))
    out = pl.pallas_call(
        functools.partial(sum_kernel, groups, owners),
        out_shape=jax.ShapeDtypeStruct(shape, jnp.float32),
        in_specs=[vmem],
        out_specs=vmem,
        scratch_shapes=[
            pltpu.VMEM((groups, *shape), jnp.float32),
            pltpu.VMEM((owners, *shape), jnp.float32),
            pltpu.SemaphoreType.DMA((copies,)),
            pltpu.SemaphoreType.DMA((copies,)),
        ],
        compiler_params=pltpu.CompilerParams(collective_id=2, has_side_effects=True),
    )(jnp.broadcast_to(rows[:, None], shape))
    return [out[k, 0] for k in range(len(values))]


def gather_kernel(groups, owners, t_ref, out_ref, whole, send_sem, recv_sem):
    me = (lax.axis_index("grp"), lax.axis_index("sub"))
    g, s = me
    half = t_ref.shape[1] // 2
    core = bit_of(g, 1)
    whole[s] = t_ref[...]
    greet(groups, owners, me)
    x0 = pl.multiple_of(core * half, math.gcd(half, 16))
    at, copies, across = 0, [], []

    def start(block, peer):
        nonlocal at
        place = whole.at[block, :, pl.ds(x0, half)]
        copy = pltpu.make_async_remote_copy(
            src_ref=place,
            dst_ref=place,
            send_sem=send_sem.at[at],
            recv_sem=recv_sem.at[at],
            device_id=peer,
            device_id_type=MESH,
        )
        copy.start()
        copies.append(copy)
        at += 1
        return copy

    def flipped(pattern):
        return s + sum(b * (1 - 2 * bit_of(s, b)) for b in bits(owners) if pattern & b)

    held = [0]
    for bit in reversed(bits(owners)):
        started = [start(flipped(p), (g, flipped(bit))) for p in held]
        for p, copy in zip(held, started):
            copy.wait_recv()
            across.append(start(flipped(p | bit), (g + 1 - 2 * core, s)))
        held = held + [p | bit for p in held]
    for copy in across:
        copy.wait_recv()
    out_ref[...] = whole[...]
    for copy in copies:
        copy.wait_send()


def gathered(template):
    groups, owners = lax.axis_size("grp"), lax.axis_size("sub")
    vmem = pl.BlockSpec(memory_space=pltpu.VMEM)
    shape = (owners, *template.shape)
    copies = 2 * (owners - 1)
    return pl.pallas_call(
        functools.partial(gather_kernel, groups, owners),
        out_shape=jax.ShapeDtypeStruct(shape, template.dtype),
        in_specs=[vmem],
        out_specs=vmem,
        scratch_shapes=[
            pltpu.VMEM(shape, template.dtype),
            pltpu.SemaphoreType.DMA((copies,)),
            pltpu.SemaphoreType.DMA((copies,)),
        ],
        compiler_params=pltpu.CompilerParams(
            collective_id=3, has_side_effects=True, vmem_limit_bytes=32 * 2**20
        ),
    )(template).reshape(-1, *template.shape[1:])


def on_device(template, subjects):
    image = gathered(template)
    depth, height, width = image.shape
    slab = template.shape[0]
    subject_count = subjects.shape[0] * lax.axis_size("grp") * lax.axis_size("sub")
    cell_count = depth * height * width
    total, image_sum, cc = reduced(image, subjects[0])
    cc_local = jnp.sum(cc)
    padded_mean = image_sum / subject_count
    mean_image = padded_mean[1:-1]

    reach = REACH + 1
    padded = jnp.pad(image, ((reach, reach), (0, 0), (0, 0)))
    near = lax.dynamic_slice_in_dim(padded, lax.axis_index("sub") * slab, slab + 2 * reach, axis=0)
    near = jnp.pad(near.astype(jnp.float32), ((0, 0), (1, 1), (1, 1)))
    slopes = (
        (near[2:, 1:-1, 1:-1] - near[:-2, 1:-1, 1:-1]) * 0.5,
        (near[1:-1, 2:, 1:-1] - near[1:-1, :-2, 1:-1]) * 0.5,
        (near[1:-1, 1:-1, 2:] - near[1:-1, 1:-1, :-2]) * 0.5,
    )
    weights = gauss_weights(REACH)
    along_z = []
    for slope in slopes:
        force = total * slope
        along_z.append(sum(w * force[o : o + slab] for o, w in enumerate(weights)))
    smooth = jnp.stack(along_z, axis=1)
    gauss_x = band_matrix(height, REACH, True)
    gauss_y = band_matrix(width, REACH, True)
    smooth = jnp.einsum(
        "zcxb,ba->zcxa", smooth, gauss_y, precision=HIGH, preferred_element_type=jnp.float32
    )
    smooth = jnp.einsum(
        "ab,zcby->zcay", gauss_x, smooth, precision=HIGH, preferred_element_type=jnp.float32
    )
    mean_velocity = smooth / subject_count
    velocity_square = jnp.sum(mean_velocity * mean_velocity)
    image_square = jnp.sum(mean_image * mean_image)
    groups = lax.axis_size("grp")
    sums = summed([cc_local, velocity_square / groups, image_square / groups])
    velocity_norm = jnp.sqrt(sums[1] / cell_count + EPSILON)
    image_norm = jnp.sqrt(sums[2] / cell_count + EPSILON)
    velocity = STEP_LENGTH * mean_velocity / velocity_norm
    slope_z = (padded_mean[2:] - padded_mean[:-2]) * 0.5
    padded_x = jnp.pad(mean_image, ((0, 0), (1, 1), (0, 0)))
    slope_x = (padded_x[:, 2:] - padded_x[:, :-2]) * 0.5
    padded_y = jnp.pad(mean_image, ((0, 0), (0, 0), (1, 1)))
    slope_y = (padded_y[:, :, 2:] - padded_y[:, :, :-2]) * 0.5
    advected = velocity[:, 0] * slope_z + velocity[:, 1] * slope_x + velocity[:, 2] * slope_y
    new_template = (mean_image - advected) / image_norm
    similarity = sums[0] / (subject_count * cell_count)
    return (velocity, new_template, similarity)


def solution(mesh):
    placed = (P("sub", None, None), P(("grp", "sub"), None, None, None))
    return jax.shard_map(
        on_device,
        mesh=mesh,
        in_specs=placed,
        out_specs=(P("sub", None, None, None), P("sub", None, None), P()),
        check_vma=False,
    )
```
